32 devices in a mesh: groups: 2 (over y), neuron: 4 (over z), row: 2 (over x), sub: 2 (over core).
Axes of the slice: x: 2, y: 2, z: 4, core: 2. Of those that a mesh axis runs over, the one named last changes fastest.
Arguments:
- features: bfloat16 [896, 9216], P(('groups', 'row', 'sub'), 'neuron'), parts along dimension 0, may hold values from -6 to 6
- ln_gain: bfloat16 [9216], P('neuron'), may hold values from 0.099609375 to 1.8984375
- up_weight: bfloat16 [9216, 4608], P(('row', 'sub'), 'neuron'), may hold values from -0.0625 to 0.0625
- up_bias: bfloat16 [4608], P('neuron'), may hold values from -3 to 3
- down_weight: bfloat16 [9216, 4608], P(('row', 'sub'), 'neuron'), may hold values from -0.1875 to 0.1875
- pred_in: bfloat16 [9216, 1024], P(None, 'neuron'), may hold values from -0.0625 to 0.0625
- pred_out: bfloat16 [1024, 36], P('neuron'), may hold values from -0.1875 to 0.1875
- active: int32 [8, 8], P('groups'), parts along dimension 0, may hold values from 0 to 35, as said below
- counts: int32 [8], P('groups'), parts along dimension 0, may hold values from 2 to 8
Outputs:
- mixed: bfloat16 [896, 9216], P(('groups', 'row', 'sub'), 'neuron'), parts along dimension 0
The draws below stay inside these ranges and needn't reach their ends.
There are 2 independent parts, one for each index of `groups`. The reference program is written for one: setup_inputs(seed, part) draws one part's arguments, and reference() takes and returns one part's arrays. A program takes and returns all parts, laid end to end along the dimension named above; an argument that names none is the same for every part. Nothing has to cross between parts.
Inputs may be any that keep to these rules, and one draw needn't show every extreme that they name: `active`: for every row group the entries before its count are distinct block ids, at most 2 of them in any one neuron range of 9 consecutive ids, and every group has a range with exactly 2; entries from its count on are arbitrary block ids.
All inputs are finite; a program needn't handle non-finite values.
Results may differ from the reference program's by a relative error of at most 0.0065.
Values may be sent and summed in bfloat16 or wider, within the bound.
A program may use at most 128 MiB of HBM per device.

```python
import jax
import jax.numpy as jnp
from jax import lax

D = 9216
BW = 128
BLK_N = 9
CAP = 2
RANK = 1024
RG = 112
NGROUP = 4
ROWS = 448
FFB = 36
FF = 4608
N_NEURON = 4


def draw_lists(key):
    listed = N_NEURON * CAP
    per = jax.random.randint(jax.random.fold_in(key, 11), (NGROUP, N_NEURON), 0, CAP + 1)
    forced = jax.random.randint(jax.random.fold_in(key, 12), (NGROUP,), 0, N_NEURON)
    ranges = jnp.arange(N_NEURON)[None, :]
    at_forced = ranges == forced[:, None]
    per = jnp.where(at_forced, CAP, per)
    full_group = jax.random.randint(jax.random.fold_in(key, 16), (), 0, NGROUP)
    offset = jax.random.randint(jax.random.fold_in(key, 17), (), 1, NGROUP)
    least_group = (full_group + offset) % NGROUP
    group_ids = jnp.arange(NGROUP)[:, None]
    per = jnp.where(group_ids == full_group, CAP, per)
    per = jnp.where(group_ids == least_group, jnp.where(at_forced, CAP, 0), per)
    mixing = jax.vmap(lambda k: jax.random.permutation(k, BLK_N))(jax.random.split(jax.random.fold_in(key, 13), NGROUP * N_NEURON))
    mixing = mixing.reshape(NGROUP, N_NEURON, BLK_N)
    ids = jnp.arange(N_NEURON)[None, :, None] * BLK_N + mixing[:, :, :CAP]
    live = jnp.arange(CAP)[None, None, :] < per[:, :, None]
    ids = ids.reshape(NGROUP, listed)
    live = live.reshape(NGROUP, listed)
    order_keys = jax.vmap(lambda k: jax.random.permutation(k, listed))(jax.random.split(jax.random.fold_in(key, 14), NGROUP))
    sort_keys = jnp.where(live, order_keys, listed + order_keys)
    order = jnp.argsort(sort_keys, axis=1, stable=True)
    sorted_ids = jnp.take_along_axis(ids, order, axis=1)
    totals = jnp.sum(live.astype(jnp.int32), axis=1)
    filler = jax.random.randint(jax.random.fold_in(key, 15), (NGROUP, listed), 0, N_NEURON * BLK_N)
    position = jnp.arange(listed)[None, :]
    active = jnp.where(position < totals[:, None], sorted_ids, filler)
    return (active.astype(jnp.int32), totals.astype(jnp.int32))


def draw_active(key, part):
    return draw_lists(key)[0]


def draw_counts(key, part):
    return draw_lists(key)[1]


def level_of(own_key, shape, cuts, least, largest):
    def one(dim, blocks):
        steps = jax.random.uniform(jax.random.fold_in(jax.random.fold_in(own_key, 6), dim), (blocks,), jnp.float32, least / len(cuts), largest / len(cuts))
        return jnp.repeat(jnp.exp(steps), shape[dim] // blocks).reshape((-1,) + (1,) * (len(shape) - dim - 1))

    factor_of = one(*cuts[0])
    for cut in cuts[1:]:
        factor_of = factor_of * one(*cut)
    return factor_of


def noise(key, shape, scale, most, pieces=(), kind=jnp.bfloat16):
    factor_of = level_of(key, shape, pieces, -0.22, 0.18) if pieces else 1.0
    drawn = jax.random.normal(key, shape, jnp.float32) * scale * factor_of
    return jnp.minimum(jnp.maximum(drawn, -most), most).astype(kind)


def setup_inputs(seed: int = 0, part: int = 0) -> dict:
    arg_keys = jax.random.split(jax.random.key(seed), 10)
    own_keys = jax.random.split(jax.random.fold_in(arg_keys[9], part), 10)
    features = noise(own_keys[0], (ROWS, D), 1.0, 6.0, ((0, 4), (1, 4)))
    ln_gain = jnp.clip(1.0 + 0.18 * jax.random.normal(arg_keys[1], (D,), jnp.float32), 0.099609375, 1.8984375).astype(jnp.bfloat16)
    up_weight = noise(arg_keys[2], (D, FF), D ** -0.5, 0.0625, ((0, 4), (1, 4)))
    up_bias = noise(arg_keys[3], (FF,), 0.5, 3.0, ((0, 4),))
    down_weight = noise(arg_keys[4], (D, FF), 1024 ** -0.5, 0.1875, ((0, 4), (1, 4)))
    pred_in = noise(arg_keys[5], (D, RANK), D ** -0.5, 0.0625, ((1, 4),))
    pred_out = noise(arg_keys[6], (RANK, FFB), RANK ** -0.5, 0.1875, ((0, 4),))
    active = draw_active(jax.random.fold_in(jax.random.fold_in(arg_keys[9], part), 71), part)
    counts = draw_counts(jax.random.fold_in(jax.random.fold_in(arg_keys[9], part), 71), part)
    return dict(features=features, ln_gain=ln_gain, up_weight=up_weight, up_bias=up_bias, down_weight=down_weight, pred_in=pred_in, pred_out=pred_out, active=active, counts=counts)


def layer_norm(rows, gain):
    values = rows.astype(jnp.float32)
    mean = lax.optimization_barrier(jnp.mean(values, axis=1, keepdims=True))
    spread = lax.optimization_barrier(jnp.mean(values * values, axis=1, keepdims=True)) - mean * mean
    scaled = (values - mean) * lax.rsqrt(spread + 1e-05) * gain.astype(jnp.float32)
    return scaled.astype(jnp.bfloat16)

def slot_ids(active, counts):
    groups, listed = active.shape
    total_blocks = N_NEURON * BLK_N
    live = jnp.arange(listed, dtype=jnp.int32)[None, :] < counts[:, None]
    catalog = jnp.arange(total_blocks, dtype=jnp.int32)
    chosen = jnp.any((active[:, :, None] == catalog[None, None, :]) & live[:, :, None], axis=1).astype(jnp.int32)
    chosen = chosen.reshape(groups, N_NEURON, BLK_N)
    order = jnp.cumsum(chosen, axis=2) - 1
    within = jnp.arange(BLK_N, dtype=jnp.int32)
    slots = jnp.arange(CAP, dtype=jnp.int32)
    hits = (order[:, :, None, :] == slots[None, None, :, None]) & (chosen[:, :, None, :] == 1)
    position = lax.optimization_barrier(jnp.sum(jnp.where(hits, within[None, None, None, :], 0), axis=3)).astype(jnp.int32)
    valid = jnp.any(hits, axis=3)
    ids = jnp.arange(N_NEURON, dtype=jnp.int32)[None, :, None] * BLK_N + position
    return (ids.reshape(groups, -1).astype(jnp.int32), valid.reshape(groups, -1))

def reference(features, ln_gain, up_weight, up_bias, down_weight, pred_in, pred_out, active, counts):
    groups = counts.shape[0]
    up_table = up_weight.reshape(D, N_NEURON * BLK_N, BW)
    down_table = down_weight.reshape(D, N_NEURON * BLK_N, BW)
    bias_table = up_bias.reshape(N_NEURON * BLK_N, BW)
    ids, valid = slot_ids(active, counts)

    def one_group(index):
        rows = lax.dynamic_slice_in_dim(features, index * RG, RG, 0)
        normed = layer_norm(rows, ln_gain)
        factor = jnp.dot(normed, pred_in, preferred_element_type=jnp.float32).astype(jnp.bfloat16)
        scores = jnp.dot(factor, pred_out, preferred_element_type=jnp.float32)
        picked = ids[index]
        live = valid[index].astype(jnp.float32)
        gate = jnp.take(jax.nn.sigmoid(scores), picked, axis=1) * live[None, :]
        up_cols = jnp.take(up_table, picked, axis=1).reshape(D, -1)
        pre = jnp.dot(normed, up_cols, preferred_element_type=jnp.float32).reshape(RG, -1, BW)
        pre = pre + jnp.take(bias_table, picked, axis=0).astype(jnp.float32)[None]
        hidden = (jax.nn.relu(pre) * gate[:, :, None]).astype(jnp.bfloat16)
        hidden = lax.optimization_barrier(hidden)
        hidden = hidden.reshape(RG, N_NEURON, CAP * BW).astype(jnp.float32)
        down_cols = jnp.take(down_table, picked, axis=1).reshape(D, N_NEURON, CAP * BW).astype(jnp.float32)
        partial_value = jnp.einsum('rnk,dnk->nrd', hidden, down_cols).astype(jnp.bfloat16)
        partial_value = lax.optimization_barrier(partial_value).astype(jnp.float32)
        return (rows.astype(jnp.float32) + lax.optimization_barrier(jnp.sum(partial_value, axis=0))).astype(jnp.bfloat16)
    mixed = lax.map(one_group, jnp.arange(groups).astype(jnp.int32))
    return mixed.reshape(groups * RG, D)
```

```python
import jax
import jax.numpy as jnp
from jax import lax
from jax.experimental import pallas as pl
from jax.experimental.pallas import tpu as pltpu
from jax.sharding import PartitionSpec as P

BW = 128
CAP = 2


epsilon = 1e-05


def normalize(values, gain, width_all, total, square):
    mean = total / width_all
    spread = square / width_all - mean * mean
    return ((values - mean) * lax.rsqrt(spread + epsilon) * gain.astype(jnp.float32)).astype(
        jnp.bfloat16
    )


def per_device(
    features, ln_gain, up_weight, up_bias, down_weight, pred_in, pred_out, active, counts
):
    group_count = lax.axis_size(("row", "sub"))
    neuron = lax.axis_index("neuron")
    group = lax.axis_index(("row", "sub"))
    slice_rows = up_weight.shape[0]
    blocks = up_weight.shape[1] // BW
    whole, gain_all = (
        lax.all_gather(features, "neuron", axis=1, tiled=True),
        lax.all_gather(ln_gain, "neuron", axis=0, tiled=True),
    )
    values = whole.astype(jnp.float32)
    normed = normalize(
        values,
        gain_all,
        values.shape[1],
        jnp.sum(values, axis=1, keepdims=True),
        jnp.sum(values * values, axis=1, keepdims=True),
    )
    factor = jnp.dot(normed, pred_in, preferred_element_type=jnp.float32).astype(jnp.bfloat16)
    terms = jnp.dot(factor, pred_out, preferred_element_type=jnp.float32)
    scores = lax.psum_scatter(
        terms.astype(jnp.bfloat16), "neuron", scatter_dimension=1, tiled=True
    ).astype(jnp.float32)
    gates = jax.nn.sigmoid(scores)
    live = lax.broadcasted_iota(jnp.int32, active.shape, 1) < counts[:, None]
    local_ids = neuron * blocks + jnp.arange(blocks, dtype=jnp.int32)
    chosen = jnp.any(
        (active[:, :, None] == local_ids[None, None, :]) & live[:, :, None], axis=1
    ).astype(jnp.int32)
    order = jnp.cumsum(chosen, axis=1) - 1
    slots = jnp.arange(CAP, dtype=jnp.int32)
    picks = ((order[:, None, :] == slots[None, :, None]) & (chosen[:, None, :] == 1)).astype(
        jnp.bfloat16
    )
    mine = lax.dynamic_index_in_dim(picks, group, 0, keepdims=False).astype(jnp.float32)
    bias_table = up_bias.reshape(blocks, BW).astype(jnp.float32)
    bias_slots = jnp.sum(mine[:, :, None] * bias_table[None, :, :], axis=1)
    gate_slots = jnp.sum(gates[:, None, :] * mine[None, :, :], axis=2)
    up_local = up_weight.reshape(slice_rows, blocks, BW)
    down_local = down_weight.reshape(slice_rows, blocks, BW)
    paired = jnp.stack((up_local, down_local), 0)
    outgoing = jnp.einsum(
        "gsj,pdjc->gspdc", picks, paired, preferred_element_type=jnp.float32
    ).astype(jnp.bfloat16)
    received = lax.all_to_all(
        outgoing[:, :, :, None], ("row", "sub"), split_axis=0, concat_axis=3, tiled=True
    )
    weights_in = received.reshape(CAP, 2, slice_rows * group_count, BW)
    pre = jnp.einsum("rd,sdc->rsc", normed, weights_in[:, 0], preferred_element_type=jnp.float32)
    hidden = (jax.nn.relu(pre + bias_slots[None]) * gate_slots[:, :, None]).astype(jnp.bfloat16)
    partial_value = jnp.einsum(
        "rsc,sdc->rd", hidden, weights_in[:, 1], preferred_element_type=jnp.float32
    )
    summed = lax.psum_scatter(
        partial_value.astype(jnp.bfloat16), "neuron", scatter_dimension=1, tiled=True
    ).astype(jnp.float32)
    return (features.astype(jnp.float32) + summed).astype(jnp.bfloat16)

N = 4
PARTS = ((0, 64), (64, 48))
MESH = pl.DeviceIdType.MESH


def layer_kernel(
    ids, x_ref, gain_ref, bias_ref, pick_ref, pout_ref, up_hbm, down_hbm, pin_hbm, out_ref,
    zbuf, zgain, xin, stats, terms, term_out, pre_out, pre_in, hid, outp, pbuf, rbuf,
    up_v, down_v, pin_v,
    z_ss, z_rs, g_ss, g_rs, x_ss, x_rs, s_ss, s_rs, t_ss, t_rs, p_ss, p_rs, h_ss, h_rs,
    o_ss, o_rs, r_ss, r_rs, w_sem,
):
    n = lax.axis_index("neuron")
    g = lax.axis_index("row") * 2 + lax.axis_index("sub")
    slice_w = x_ref.shape[1]
    full = slice_w * N
    f32, bf16 = jnp.float32, jnp.bfloat16

    def zdev(m):
        return {"neuron": m}

    def pdev(w):
        return {"row": w // 2, "sub": lax.rem(w, 2)}

    def send(src, dst, ss, rs, dev):
        return pltpu.make_async_remote_copy(
            src_ref=src, dst_ref=dst, send_sem=ss, recv_sem=rs, device_id=dev, device_id_type=MESH
        )

    blocks = up_v.shape[0]
    loads = [[pltpu.make_async_copy(pin_hbm, pin_v, w_sem.at[0, 0])]]
    for i, (a, b) in enumerate(((up_hbm, up_v), (down_hbm, down_v))):
        loads.append(
            [
                pltpu.make_async_copy(a.at[:, pl.ds(j * BW, BW)], b.at[j], w_sem.at[1 + i, j])
                for j in range(blocks)
            ]
        )
    for group in loads:
        for load in group:
            load.start()
    zpeer = [lax.rem(n + k, N) for k in range(N)]
    ppeer = [lax.rem(g + k, N) for k in range(N)]
    barrier = pltpu.get_barrier_semaphore()
    for k in range(1, N):
        pl.semaphore_signal(barrier, inc=1, device_id=zdev(zpeer[k]), device_id_type=MESH)
        pl.semaphore_signal(barrier, inc=1, device_id=pdev(ppeer[k]), device_id_type=MESH)
    pl.semaphore_wait(barrier, 2 * (N - 1))

    sent = []

    def go(copy):
        copy.start()
        sent.append(copy)

    def rows(c):
        return pl.ds(PARTS[c][0], PARTS[c][1])

    chunks = range(len(PARTS))
    for c in chunks:
        for k in range(1, N):
            go(send(x_ref.at[rows(c)], zbuf.at[n, rows(c)], z_ss.at[k, c], z_rs.at[n, c], zdev(zpeer[k])))
            if c == 0:
                go(send(gain_ref, zgain.at[n], g_ss.at[k], g_rs.at[n], zdev(zpeer[k])))
    zbuf[n] = x_ref[...]
    zgain[n] = gain_ref[...]

    for c in chunks:
        for k in (1, 2, 3, 0):
            w = ppeer[k]

            @pl.when(w != n)
            def _(w=w, c=c):
                send(x_ref.at[rows(c)], zbuf.at[w, rows(c)], z_ss.at[1, c], z_rs.at[w, c], zdev(zpeer[1])).wait_recv()

            if k:
                go(send(zbuf.at[w, rows(c)], xin.at[g, rows(c)], x_ss.at[k, c], x_rs.at[g, c], pdev(w)))
    for k in range(1, N):
        m = zpeer[k]
        send(gain_ref, zgain.at[m], g_ss.at[1], g_rs.at[m], zdev(m)).wait_recv()

    def add_stats(m, carry):
        total, square = carry
        v = zbuf[m].astype(f32)
        return (
            total + jnp.sum(v, axis=1, keepdims=True),
            square + jnp.sum(v * v, axis=1, keepdims=True),
        )

    zero = jnp.zeros((x_ref.shape[0], 1), f32)
    total, square = lax.fori_loop(0, N, add_stats, (zero, zero))
    mean = total / full
    scale = lax.rsqrt(square / full - mean * mean + epsilon)
    lane = lax.broadcasted_iota(jnp.int32, (x_ref.shape[0], 128), 1)
    stats[g] = jnp.where(lane < 64, mean, scale)
    for k in range(1, N):
        go(send(stats.at[g], stats.at[g], s_ss.at[k], s_rs.at[g], pdev(ppeer[k])))

    def norm(values, mu, sc, gain):
        return ((values.astype(f32) - mu) * sc * gain).astype(bf16)

    for load in loads[0]:
        load.wait()

    def add_factor(m, acc):
        block = pin_v[pl.ds(pl.multiple_of(m * slice_w, 128), slice_w), :]
        return acc + jnp.dot(norm(zbuf[m], mean, scale, zgain[m]), block, preferred_element_type=f32)

    factor = lax.fori_loop(0, N, add_factor, jnp.zeros((x_ref.shape[0], pin_v.shape[1]), f32))
    term_out[...] = jnp.dot(factor.astype(bf16), pout_ref[...], preferred_element_type=f32).astype(bf16)
    terms[n] = term_out[...]
    for k in range(1, N):
        go(send(term_out, terms.at[n], t_ss.at[k], t_rs.at[n], zdev(zpeer[k])))

    def picked(ref, q):
        return jnp.concatenate((ref[ids[2 * q]], ref[ids[2 * q + 1]]), axis=1)

    for load in loads[1]:
        load.wait()
    xin[g] = zbuf[g]

    def up(k, _):
        q = lax.rem(g + k, N)

        @pl.when(k < N)
        def _():
            for c in chunks:
                send(x_ref.at[rows(c)], xin.at[q, rows(c)], x_ss.at[1, c], x_rs.at[q, c], pdev(q)).wait_recv()
            send(stats.at[g], stats.at[q], s_ss.at[1], s_rs.at[q], pdev(q)).wait_recv()

        st = stats[q]
        normed = norm(xin[q], st[:, 0:1], st[:, 64:65], zgain[g])
        pre = jnp.dot(normed, picked(up_v, q), preferred_element_type=f32)
        pre_out[q] = pre.astype(bf16)

        @pl.when(k < N)
        def _():
            send(pre_out.at[q], pre_in.at[g], p_ss.at[lax.rem(k, N)], p_rs.at[g], pdev(q)).start()

        return 0

    lax.fori_loop(1, N + 1, up, 0)
    for k in range(1, N):
        sent.append(send(pre_out.at[ppeer[k]], pre_in.at[g], p_ss.at[k], p_rs.at[g], pdev(ppeer[k])))

    for k in range(1, N):
        m = zpeer[k]
        send(term_out, terms.at[m], t_ss.at[1], t_rs.at[m], zdev(m)).wait_recv()
    scores = jnp.zeros((x_ref.shape[0], 128), f32)
    for m in range(N):
        scores = scores + terms[m].astype(f32)
    gates = jax.nn.sigmoid(scores)
    gate = [jnp.sum(gates * pick_ref[j], axis=1, keepdims=True) for j in range(CAP)]
    pre = pre_out[g].astype(f32)
    for k in range(1, N):
        q = ppeer[k]
        send(pre_out.at[g], pre_in.at[q], p_ss.at[1], p_rs.at[q], pdev(q)).wait_recv()
        pre = pre + pre_in[q].astype(f32)
    hidden = [
        (jnp.maximum(pre[:, j * BW : (j + 1) * BW] + bias_ref[j], 0.0) * gate[j]).astype(bf16)
        for j in range(2)
    ]
    hid[g] = jnp.concatenate(hidden, axis=1)
    for k in range(1, N):
        go(send(hid.at[g], hid.at[g], h_ss.at[k], h_rs.at[g], pdev(ppeer[k])))

    for load in loads[2]:
        load.wait()

    def down(k, _):
        q = lax.rem(g + k, N)

        @pl.when(k < N)
        def _():
            send(hid.at[g], hid.at[q], h_ss.at[1], h_rs.at[q], pdev(q)).wait_recv()

        outp[q] = lax.dot_general(
            hid[q], picked(down_v, q), (((1,), (1,)), ((), ())), preferred_element_type=f32
        ).astype(bf16)

        @pl.when(k < N)
        def _():
            for c in chunks:
                send(outp.at[q, rows(c)], pbuf.at[g, rows(c)], o_ss.at[lax.rem(k, N), c], o_rs.at[g, c], pdev(q)).start()

        return 0

    lax.fori_loop(1, N + 1, down, 0)
    for k in range(1, N):
        for c in chunks:
            sent.append(send(outp.at[ppeer[k], rows(c)], pbuf.at[g, rows(c)], o_ss.at[k, c], o_rs.at[g, c], pdev(ppeer[k])))
    pbuf[g] = outp[g]
    for c in chunks:
        for k in (1, 2, 3, 0):
            m = zpeer[k]

            @pl.when(m != g)
            def _(m=m, c=c):
                send(outp.at[0, rows(c)], pbuf.at[m, rows(c)], o_ss.at[1, c], o_rs.at[m, c], pdev(ppeer[1])).wait_recv()

            if k:
                go(send(pbuf.at[m, rows(c)], rbuf.at[n, rows(c)], r_ss.at[k, c], r_rs.at[n, c], zdev(m)))
    for c in chunks:
        acc = pbuf[n, rows(c)].astype(f32)
        for k in range(1, N):
            m = zpeer[k]
            send(pbuf.at[m, rows(c)], rbuf.at[m, rows(c)], r_ss.at[1, c], r_rs.at[m, c], zdev(m)).wait_recv()
            acc = acc + rbuf[m, rows(c)].astype(f32)
        out_ref[rows(c)] = (x_ref[rows(c)].astype(f32) + acc).astype(bf16)
    for copy in sent:
        copy.wait_send()


def fused_device(
    features, ln_gain, up_weight, up_bias, down_weight, pred_in, pred_out, active, counts
):
    neuron = lax.axis_index("neuron")
    blocks = up_weight.shape[1] // BW
    height, slice_w = features.shape
    live = lax.broadcasted_iota(jnp.int32, active.shape, 1) < counts[:, None]
    local_ids = neuron * blocks + jnp.arange(blocks, dtype=jnp.int32)
    chosen = jnp.any((active[:, :, None] == local_ids[None, None, :]) & live[:, :, None], axis=1)
    number = jnp.arange(blocks, dtype=jnp.int32)[None, :]
    lowest = jnp.min(jnp.where(chosen, number, blocks), axis=1)
    highest = jnp.max(jnp.where(chosen, number, -1), axis=1)
    places = jnp.stack((jnp.minimum(lowest, blocks - 1), jnp.maximum(highest, 0)), axis=1)
    group = lax.axis_index(("row", "sub"))
    mine = lax.dynamic_index_in_dim(places, group, 0, keepdims=False)
    low = lax.dynamic_index_in_dim(lowest, group, 0, keepdims=False)
    high = lax.dynamic_index_in_dim(highest, group, 0, keepdims=False)
    valid = jnp.stack((high >= 0, high > low))
    lanes = jnp.arange(128, dtype=jnp.int32)[None, :]
    pick = ((lanes == neuron * blocks + mine[:, None]) & valid[:, None]).astype(jnp.float32)[:, None]
    hot = (number == mine[:, None]).astype(jnp.float32)
    bias_table = up_bias.reshape(blocks, BW).astype(jnp.float32)
    bias = jnp.sum(hot[:, :, None] * bias_table[None], axis=1)[:, None]
    gain = ln_gain.astype(jnp.float32).reshape(1, slice_w)
    pout = jnp.pad(pred_out, ((0, 0), (0, 128 - pred_out.shape[1])))
    vmem = pl.BlockSpec(memory_space=pltpu.VMEM)
    hbm = pl.BlockSpec(memory_space=pl.ANY)
    nc = len(PARTS)
    bf16, f32 = jnp.bfloat16, jnp.float32
    dma = pltpu.SemaphoreType.DMA
    return pl.pallas_call(
        layer_kernel,
        out_shape=jax.ShapeDtypeStruct(features.shape, bf16),
        in_specs=[pl.BlockSpec(memory_space=pltpu.SMEM)] + [vmem] * 5 + [hbm] * 3,
        out_specs=vmem,
        scratch_shapes=[
            pltpu.VMEM((N, height, slice_w), bf16),
            pltpu.VMEM((N, 1, slice_w), f32),
            pltpu.VMEM((N, height, slice_w), bf16),
            pltpu.VMEM((N, height, 128), f32),
            pltpu.VMEM((N, height, 128), bf16),
            pltpu.VMEM((height, 128), bf16),
            pltpu.VMEM((N, height, CAP * BW), bf16),
            pltpu.VMEM((N, height, CAP * BW), bf16),
            pltpu.VMEM((N, height, CAP * BW), bf16),
            pltpu.VMEM((N, height, slice_w), bf16),
            pltpu.VMEM((N, height, slice_w), bf16),
            pltpu.VMEM((N, height, slice_w), bf16),
            pltpu.VMEM((blocks, up_weight.shape[0], BW), bf16),
            pltpu.VMEM((blocks, down_weight.shape[0], BW), bf16),
            pltpu.VMEM(pred_in.shape, bf16),
            dma((N, nc)), dma((N, nc)),
            dma((N,)), dma((N,)),
            dma((N, nc)), dma((N, nc)),
            dma((N,)), dma((N,)),
            dma((N,)), dma((N,)),
            dma((N,)), dma((N,)),
            dma((N,)), dma((N,)),
            dma((N, nc)), dma((N, nc)),
            dma((N, nc)), dma((N, nc)),
            dma((3, blocks)),
        ],
        compiler_params=pltpu.CompilerParams(
            collective_id=0, has_side_effects=True, vmem_limit_bytes=50 * 1024 * 1024
        ),
    )(places.reshape(-1), features, gain, bias, pick, pout, up_weight, down_weight, pred_in)


def solution(mesh):
    placed = (
        P(("groups", "row", "sub"), "neuron"),
        P("neuron"),
        P(("row", "sub"), "neuron"),
        P("neuron"),
        P(("row", "sub"), "neuron"),
        P(None, "neuron"),
        P("neuron", None),
        P("groups", None),
        P("groups"),
    )
    small = mesh.shape["neuron"] == N and mesh.shape["row"] == 2 and mesh.shape["sub"] == 2
    return jax.shard_map(
        fused_device if small else per_device,
        mesh=mesh,
        in_specs=placed,
        out_specs=P(("groups", "row", "sub"), "neuron"),
        check_vma=False,
    )
```

```python
import jax
import jax.numpy as jnp
from jax import lax
from jax.experimental import pallas as pl
from jax.experimental.pallas import tpu as pltpu
from jax.sharding import PartitionSpec as P

BW = 128
CAP = 2


epsilon = 1e-05


def normalize(values, gain, width_all, total, square):
    mean = total / width_all
    spread = square / width_all - mean * mean
    return ((values - mean) * lax.rsqrt(spread + epsilon) * gain.astype(jnp.float32)).astype(
        jnp.bfloat16
    )


def per_device(
    features, ln_gain, up_weight, up_bias, down_weight, pred_in, pred_out, active, counts
):
    group_count = lax.axis_size(("row", "sub"))
    neuron = lax.axis_index("neuron")
    group = lax.axis_index(("row", "sub"))
    slice_rows = up_weight.shape[0]
    blocks = up_weight.shape[1] // BW
    whole, gain_all = (
        lax.all_gather(features, "neuron", axis=1, tiled=True),
        lax.all_gather(ln_gain, "neuron", axis=0, tiled=True),
    )
    values = whole.astype(jnp.float32)
    normed = normalize(
        values,
        gain_all,
        values.shape[1],
        jnp.sum(values, axis=1, keepdims=True),
        jnp.sum(values * values, axis=1, keepdims=True),
    )
    factor = jnp.dot(normed, pred_in, preferred_element_type=jnp.float32).astype(jnp.bfloat16)
    terms = jnp.dot(factor, pred_out, preferred_element_type=jnp.float32)
    scores = lax.psum_scatter(
        terms.astype(jnp.bfloat16), "neuron", scatter_dimension=1, tiled=True
    ).astype(jnp.float32)
    gates = jax.nn.sigmoid(scores)
    live = lax.broadcasted_iota(jnp.int32, active.shape, 1) < counts[:, None]
    local_ids = neuron * blocks + jnp.arange(blocks, dtype=jnp.int32)
    chosen = jnp.any(
        (active[:, :, None] == local_ids[None, None, :]) & live[:, :, None], axis=1
    ).astype(jnp.int32)
    order = jnp.cumsum(chosen, axis=1) - 1
    slots = jnp.arange(CAP, dtype=jnp.int32)
    picks = ((order[:, None, :] == slots[None, :, None]) & (chosen[:, None, :] == 1)).astype(
        jnp.bfloat16
    )
    mine = lax.dynamic_index_in_dim(picks, group, 0, keepdims=False).astype(jnp.float32)
    bias_table = up_bias.reshape(blocks, BW).astype(jnp.float32)
    bias_slots = jnp.sum(mine[:, :, None] * bias_table[None, :, :], axis=1)
    gate_slots = jnp.sum(gates[:, None, :] * mine[None, :, :], axis=2)
    up_local = up_weight.reshape(slice_rows, blocks, BW)
    down_local = down_weight.reshape(slice_rows, blocks, BW)
    paired = jnp.stack((up_local, down_local), 0)
    outgoing = jnp.einsum(
        "gsj,pdjc->gspdc", picks, paired, preferred_element_type=jnp.float32
    ).astype(jnp.bfloat16)
    received = lax.all_to_all(
        outgoing[:, :, :, None], ("row", "sub"), split_axis=0, concat_axis=3, tiled=True
    )
    weights_in = received.reshape(CAP, 2, slice_rows * group_count, BW)
    pre = jnp.einsum("rd,sdc->rsc", normed, weights_in[:, 0], preferred_element_type=jnp.float32)
    hidden = (jax.nn.relu(pre + bias_slots[None]) * gate_slots[:, :, None]).astype(jnp.bfloat16)
    partial_value = jnp.einsum(
        "rsc,sdc->rd", hidden, weights_in[:, 1], preferred_element_type=jnp.float32
    )
    summed = lax.psum_scatter(
        partial_value.astype(jnp.bfloat16), "neuron", scatter_dimension=1, tiled=True
    ).astype(jnp.float32)
    return (features.astype(jnp.float32) + summed).astype(jnp.bfloat16)

N = 4
PARTS = ((0, 32), (32, 32), (64, 32), (96, 16))
MESH = pl.DeviceIdType.MESH


def layer_kernel(
    ids, x_ref, gain_ref, bias_ref, pick_ref, pout_ref, up_hbm, down_hbm, pin_hbm, out_ref,
    zbuf, zgain, xin, stats, terms, term_out, pre_out, pre_in, hid, outp, pbuf, rup, rdn,
    up_v, down_v, pin_v,
    z_ss, z_rs, g_ss, g_rs, x_ss, x_rs, s_ss, s_rs, t_ss, t_rs, p_ss, p_rs, h_ss, h_rs,
    o_ss, o_rs, u_ss, u_rs, d_ss, d_rs, w_sem,
):
    n = lax.axis_index("neuron")
    row, sub = lax.axis_index("row"), lax.axis_index("sub")
    g = row * 2 + sub
    slice_w = x_ref.shape[1]
    full = slice_w * N
    f32, bf16 = jnp.float32, jnp.bfloat16

    def zdev(m):
        return {"neuron": m}

    def pdev(w):
        return {"row": w // 2, "sub": lax.rem(w, 2)}

    def send(src, dst, ss, rs, dev):
        return pltpu.make_async_remote_copy(
            src_ref=src, dst_ref=dst, send_sem=ss, recv_sem=rs, device_id=dev, device_id_type=MESH
        )

    blocks = up_v.shape[0]
    loads = [[pltpu.make_async_copy(pin_hbm, pin_v, w_sem.at[0, 0])]]
    for i, (a, b) in enumerate(((up_hbm, up_v), (down_hbm, down_v))):
        loads.append(
            [
                pltpu.make_async_copy(a.at[:, pl.ds(j * BW, BW)], b.at[j], w_sem.at[1 + i, j])
                for j in range(blocks)
            ]
        )
    for group in loads:
        for load in group:
            load.start()
    zpeer = [lax.rem(n + k, N) for k in range(N)]

    def plane(k):
        flip_row, flip_sub = 1 - k // 3, lax.rem(k // 2, 2)
        return 2 * (row + flip_row - 2 * row * flip_row) + sub + flip_sub - 2 * sub * flip_sub

    ppeer = [g] + [plane(jnp.int32(k)) for k in range(1, N)]
    barrier = pltpu.get_barrier_semaphore()
    for k in range(1, N):
        pl.semaphore_signal(barrier, inc=1, device_id=zdev(zpeer[k]), device_id_type=MESH)
        pl.semaphore_signal(barrier, inc=1, device_id=pdev(ppeer[k]), device_id_type=MESH)
    pl.semaphore_wait(barrier, 2 * (N - 1))

    sent = []

    def go(copy):
        copy.start()
        sent.append(copy)

    def rows(c):
        return pl.ds(PARTS[c][0], PARTS[c][1])

    chunks = range(len(PARTS))
    def hop(m, c, up, src):
        return send(
            src, zbuf.at[m, rows(c)], z_ss.at[m, c, 0 if up else 1], z_rs.at[m, c], zdev(n + 1 if up else n - 1)
        )

    def guarded(cond, fn):
        pl.when(cond)(fn)

    for c in chunks:
        guarded(n < N - 1, lambda c=c: hop(n, c, True, x_ref.at[rows(c)]).start())
        guarded(n > 0, lambda c=c: hop(n, c, False, x_ref.at[rows(c)]).start())
    for k in range(1, N):
        go(send(gain_ref, zgain.at[n], g_ss.at[k], g_rs.at[n], zdev(zpeer[k])))
    zbuf[n] = x_ref[...]
    zgain[n] = gain_ref[...]

    def inward(m, c, src):
        return send(src, xin.at[g, rows(c)], x_ss.at[m, c], x_rs.at[g, c], pdev(m))

    for c in chunks:
        guarded(n != g, lambda c=c: inward(n, c, x_ref.at[rows(c)]).start())
    for far in range(1, N):
        for c in chunks:
            for up in (True, False):
                m = n - far if up else n + far

                def arrive(m=m, c=c, up=up):
                    block = zbuf.at[m, rows(c)]
                    send(x_ref.at[rows(c)], block, z_ss.at[m, c, 0], z_rs.at[m, c], zdev(zpeer[1])).wait_recv()
                    guarded(n < N - 1 if up else n > 0, lambda: hop(m, c, up, block).start())
                    guarded(m != g, lambda: inward(m, c, block).start())

                guarded(m >= 0 if up else m < N, arrive)
    for k in range(1, N):
        m = zpeer[k]
        send(gain_ref, zgain.at[m], g_ss.at[1], g_rs.at[m], zdev(m)).wait_recv()

    def add_stats(m, carry):
        total, square = carry
        v = zbuf[m].astype(f32)
        return (
            total + jnp.sum(v, axis=1, keepdims=True),
            square + jnp.sum(v * v, axis=1, keepdims=True),
        )

    zero = jnp.zeros((x_ref.shape[0], 1), f32)
    total, square = lax.fori_loop(0, N, add_stats, (zero, zero))
    mean = total / full
    scale = lax.rsqrt(square / full - mean * mean + epsilon)
    lane = lax.broadcasted_iota(jnp.int32, (x_ref.shape[0], 128), 1)
    stats[g] = jnp.where(lane < 64, mean, scale)
    for k in range(1, N):
        go(send(stats.at[g], stats.at[g], s_ss.at[k], s_rs.at[g], pdev(ppeer[k])))

    def norm(values, mu, sc, gain):
        return ((values.astype(f32) - mu) * sc * gain).astype(bf16)

    for load in loads[0]:
        load.wait()

    def add_factor(m, acc):
        block = pin_v[pl.ds(pl.multiple_of(m * slice_w, 128), slice_w), :]
        return acc + jnp.dot(norm(zbuf[m], mean, scale, zgain[m]), block, preferred_element_type=f32)

    factor = lax.fori_loop(0, N, add_factor, jnp.zeros((x_ref.shape[0], pin_v.shape[1]), f32))
    term_out[...] = jnp.dot(factor.astype(bf16), pout_ref[...], preferred_element_type=f32).astype(bf16)
    terms[n] = term_out[...]
    for k in range(1, N):
        go(send(term_out, terms.at[n], t_ss.at[k], t_rs.at[n], zdev(zpeer[k])))

    def picked(ref, q):
        return jnp.concatenate((ref[ids[2 * q]], ref[ids[2 * q + 1]]), axis=1)

    for load in loads[1]:
        load.wait()
    xin[g] = zbuf[g]

    def up(k, _):
        q = plane(k)

        @pl.when(k < N)
        def _():
            for c in chunks:
                send(x_ref.at[rows(c)], xin.at[q, rows(c)], x_ss.at[1, c], x_rs.at[q, c], pdev(q)).wait_recv()
            send(stats.at[g], stats.at[q], s_ss.at[1], s_rs.at[q], pdev(q)).wait_recv()

        st = stats[q]
        normed = norm(xin[q], st[:, 0:1], st[:, 64:65], zgain[g])
        pre = jnp.dot(normed, picked(up_v, q), preferred_element_type=f32)
        pre_out[q] = pre.astype(bf16)

        @pl.when(k < N)
        def _():
            send(pre_out.at[q], pre_in.at[g], p_ss.at[lax.rem(k, N)], p_rs.at[g], pdev(q)).start()

        return 0

    lax.fori_loop(1, N + 1, up, 0)
    for k in range(1, N):
        sent.append(send(pre_out.at[ppeer[k]], pre_in.at[g], p_ss.at[k], p_rs.at[g], pdev(ppeer[k])))

    for k in range(1, N):
        m = zpeer[k]
        send(term_out, terms.at[m], t_ss.at[1], t_rs.at[m], zdev(m)).wait_recv()
    scores = jnp.zeros((x_ref.shape[0], 128), f32)
    for m in range(N):
        scores = scores + terms[m].astype(f32)
    gates = jax.nn.sigmoid(scores)
    gate = [jnp.sum(gates * pick_ref[j], axis=1, keepdims=True) for j in range(CAP)]
    pre = pre_out[g].astype(f32)
    for k in range(1, N):
        q = ppeer[k]
        send(pre_out.at[g], pre_in.at[q], p_ss.at[1], p_rs.at[q], pdev(q)).wait_recv()
        pre = pre + pre_in[q].astype(f32)
    hidden = [
        (jnp.maximum(pre[:, j * BW : (j + 1) * BW] + bias_ref[j], 0.0) * gate[j]).astype(bf16)
        for j in range(2)
    ]
    hid[g] = jnp.concatenate(hidden, axis=1)
    for k in range(1, N):
        go(send(hid.at[g], hid.at[g], h_ss.at[k], h_rs.at[g], pdev(ppeer[k])))

    for load in loads[2]:
        load.wait()

    def down(k, _):
        q = plane(k)

        @pl.when(k < N)
        def _():
            send(hid.at[g], hid.at[q], h_ss.at[1], h_rs.at[q], pdev(q)).wait_recv()

        outp[q] = lax.dot_general(
            hid[q], picked(down_v, q), (((1,), (1,)), ((), ())), preferred_element_type=f32
        ).astype(bf16)
        return 0

    def outward(k, c):
        q = ppeer[k]
        return send(outp.at[q, rows(c)], pbuf.at[g, rows(c)], o_ss.at[k, c], o_rs.at[g, c], pdev(q))

    lax.fori_loop(1, 3, down, 0)
    for c in chunks:
        for k in (1, 2):
            go(outward(k, c))
    lax.fori_loop(3, N + 1, down, 0)
    for c in chunks:
        go(outward(3, c))
    pbuf[g] = outp[g]

    def rise(m, c, up):
        at = pbuf.at[m, rows(c)]
        if up:
            return send(at, rup.at[m, rows(c)], u_ss.at[m, c], u_rs.at[m, c], zdev(n + 1))
        return send(at, rdn.at[m, rows(c)], d_ss.at[m, c], d_rs.at[m, c], zdev(n - 1))

    def landed(m, c, up):
        buf, sems = (rup, u_rs) if up else (rdn, d_rs)
        send(x_ref.at[rows(c)], buf.at[m, rows(c)], u_ss.at[m, c], sems.at[m, c], zdev(zpeer[1])).wait_recv()

    def own(m, c):
        def wait():
            send(outp.at[0, rows(c)], pbuf.at[m, rows(c)], o_ss.at[1, c], o_rs.at[m, c], pdev(ppeer[1])).wait_recv()

        guarded(m != g, wait)

    for c in chunks:
        for far in (3, 2, 1):
            for up in (True, False):
                m = n + far if up else n - far

                def forward(m=m, c=c, up=up):
                    own(m, c)

                    def add():
                        landed(m, c, up)
                        other = rup if up else rdn
                        pbuf[m, rows(c)] = (
                            pbuf[m, rows(c)].astype(f32) + other[m, rows(c)].astype(f32)
                        ).astype(bf16)

                    guarded(n > 0 if up else n < N - 1, add)
                    rise(m, c, up).start()

                guarded(m < N if up else m >= 0, forward)
    for c in chunks:
        own(n, c)

        def middle(c=c):
            landed(n, c, True)
            landed(n, c, False)
            total = rup[n, rows(c)].astype(f32) + rdn[n, rows(c)].astype(f32) + pbuf[n, rows(c)].astype(f32)
            out_ref[rows(c)] = (x_ref[rows(c)].astype(f32) + total).astype(bf16)

        def edge(c=c, up=True):
            landed(n, c, up)
            other = rup if up else rdn
            total = other[n, rows(c)].astype(f32) + pbuf[n, rows(c)].astype(f32)
            out_ref[rows(c)] = (x_ref[rows(c)].astype(f32) + total).astype(bf16)

        guarded(n == 0, lambda c=c: edge(c, False))
        guarded(n == N - 1, lambda c=c: edge(c, True))
        guarded((n > 0) & (n < N - 1), middle)
    for c in chunks:
        for m in range(N):
            guarded((n >= m) & (n < N - 1), lambda m=m, c=c: hop(m, c, True, x_ref.at[rows(c)]).wait_send())
            guarded((n <= m) & (n > 0), lambda m=m, c=c: hop(m, c, False, x_ref.at[rows(c)]).wait_send())
            guarded(g != m, lambda m=m, c=c: inward(m, c, x_ref.at[rows(c)]).wait_send())
            guarded(n < m, lambda m=m, c=c: rise(m, c, True).wait_send())
            guarded(n > m, lambda m=m, c=c: rise(m, c, False).wait_send())
    for copy in sent:
        copy.wait_send()


def fused_device(
    features, ln_gain, up_weight, up_bias, down_weight, pred_in, pred_out, active, counts
):
    neuron = lax.axis_index("neuron")
    blocks = up_weight.shape[1] // BW
    height, slice_w = features.shape
    live = lax.broadcasted_iota(jnp.int32, active.shape, 1) < counts[:, None]
    local_ids = neuron * blocks + jnp.arange(blocks, dtype=jnp.int32)
    chosen = jnp.any((active[:, :, None] == local_ids[None, None, :]) & live[:, :, None], axis=1)
    number = jnp.arange(blocks, dtype=jnp.int32)[None, :]
    lowest = jnp.min(jnp.where(chosen, number, blocks), axis=1)
    highest = jnp.max(jnp.where(chosen, number, -1), axis=1)
    places = jnp.stack((jnp.minimum(lowest, blocks - 1), jnp.maximum(highest, 0)), axis=1)
    group = lax.axis_index(("row", "sub"))
    mine = lax.dynamic_index_in_dim(places, group, 0, keepdims=False)
    low = lax.dynamic_index_in_dim(lowest, group, 0, keepdims=False)
    high = lax.dynamic_index_in_dim(highest, group, 0, keepdims=False)
    valid = jnp.stack((high >= 0, high > low))
    lanes = jnp.arange(128, dtype=jnp.int32)[None, :]
    pick = ((lanes == neuron * blocks + mine[:, None]) & valid[:, None]).astype(jnp.float32)[:, None]
    hot = (number == mine[:, None]).astype(jnp.float32)
    bias_table = up_bias.reshape(blocks, BW).astype(jnp.float32)
    bias = jnp.sum(hot[:, :, None] * bias_table[None], axis=1)[:, None]
    gain = ln_gain.astype(jnp.float32).reshape(1, slice_w)
    pout = jnp.pad(pred_out, ((0, 0), (0, 128 - pred_out.shape[1])))
    vmem = pl.BlockSpec(memory_space=pltpu.VMEM)
    hbm = pl.BlockSpec(memory_space=pl.ANY)
    nc = len(PARTS)
    bf16, f32 = jnp.bfloat16, jnp.float32
    dma = pltpu.SemaphoreType.DMA
    return pl.pallas_call(
        layer_kernel,
        out_shape=jax.ShapeDtypeStruct(features.shape, bf16),
        in_specs=[pl.BlockSpec(memory_space=pltpu.SMEM)] + [vmem] * 5 + [hbm] * 3,
        out_specs=vmem,
        scratch_shapes=[
            pltpu.VMEM((N, height, slice_w), bf16),
            pltpu.VMEM((N, 1, slice_w), f32),
            pltpu.VMEM((N, height, slice_w), bf16),
            pltpu.VMEM((N, height, 128), f32),
            pltpu.VMEM((N, height, 128), bf16),
            pltpu.VMEM((height, 128), bf16),
            pltpu.VMEM((N, height, CAP * BW), bf16),
            pltpu.VMEM((N, height, CAP * BW), bf16),
            pltpu.VMEM((N, height, CAP * BW), bf16),
            pltpu.VMEM((N, height, slice_w), bf16),
            pltpu.VMEM((N, height, slice_w), bf16),
            pltpu.VMEM((N, height, slice_w), bf16),
            pltpu.VMEM((N, height, slice_w), bf16),
            pltpu.VMEM((blocks, up_weight.shape[0], BW), bf16),
            pltpu.VMEM((blocks, down_weight.shape[0], BW), bf16),
            pltpu.VMEM(pred_in.shape, bf16),
            dma((N, nc, 2)), dma((N, nc)),
            dma((N,)), dma((N,)),
            dma((N, nc)), dma((N, nc)),
            dma((N,)), dma((N,)),
            dma((N,)), dma((N,)),
            dma((N,)), dma((N,)),
            dma((N,)), dma((N,)),
            dma((N, nc)), dma((N, nc)),
            dma((N, nc)), dma((N, nc)),
            dma((N, nc)), dma((N, nc)),
            dma((3, blocks)),
        ],
        compiler_params=pltpu.CompilerParams(
            collective_id=0, has_side_effects=True, vmem_limit_bytes=50 * 1024 * 1024
        ),
    )(places.reshape(-1), features, gain, bias, pick, pout, up_weight, down_weight, pred_in)


def solution(mesh):
    placed = (
        P(("groups", "row", "sub"), "neuron"),
        P("neuron"),
        P(("row", "sub"), "neuron"),
        P("neuron"),
        P(("row", "sub"), "neuron"),
        P(None, "neuron"),
        P("neuron", None),
        P("groups", None),
        P("groups"),
    )
    small = mesh.shape["neuron"] == N and mesh.shape["row"] == 2 and mesh.shape["sub"] == 2
    return jax.shard_map(
        fused_device if small else per_device,
        mesh=mesh,
        in_specs=placed,
        out_specs=P(("groups", "row", "sub"), "neuron"),
        check_vma=False,
    )
```

```python
import jax
import jax.numpy as jnp
from jax import lax
from jax.experimental import pallas as pl
from jax.experimental.pallas import tpu as pltpu
from jax.sharding import PartitionSpec as P

BW = 128
CAP = 2


epsilon = 1e-05


def normalize(values, gain, width_all, total, square):
    mean = total / width_all
    spread = square / width_all - mean * mean
    return ((values - mean) * lax.rsqrt(spread + epsilon) * gain.astype(jnp.float32)).astype(
        jnp.bfloat16
    )


def per_device(
    features, ln_gain, up_weight, up_bias, down_weight, pred_in, pred_out, active, counts
):
    group_count = lax.axis_size(("row", "sub"))
    neuron = lax.axis_index("neuron")
    group = lax.axis_index(("row", "sub"))
    slice_rows = up_weight.shape[0]
    blocks = up_weight.shape[1] // BW
    whole, gain_all = (
        lax.all_gather(features, "neuron", axis=1, tiled=True),
        lax.all_gather(ln_gain, "neuron", axis=0, tiled=True),
    )
    values = whole.astype(jnp.float32)
    normed = normalize(
        values,
        gain_all,
        values.shape[1],
        jnp.sum(values, axis=1, keepdims=True),
        jnp.sum(values * values, axis=1, keepdims=True),
    )
    factor = jnp.dot(normed, pred_in, preferred_element_type=jnp.float32).astype(jnp.bfloat16)
    terms = jnp.dot(factor, pred_out, preferred_element_type=jnp.float32)
    scores = lax.psum_scatter(
        terms.astype(jnp.bfloat16), "neuron", scatter_dimension=1, tiled=True
    ).astype(jnp.float32)
    gates = jax.nn.sigmoid(scores)
    live = lax.broadcasted_iota(jnp.int32, active.shape, 1) < counts[:, None]
    local_ids = neuron * blocks + jnp.arange(blocks, dtype=jnp.int32)
    chosen = jnp.any(
        (active[:, :, None] == local_ids[None, None, :]) & live[:, :, None], axis=1
    ).astype(jnp.int32)
    order = jnp.cumsum(chosen, axis=1) - 1
    slots = jnp.arange(CAP, dtype=jnp.int32)
    picks = ((order[:, None, :] == slots[None, :, None]) & (chosen[:, None, :] == 1)).astype(
        jnp.bfloat16
    )
    mine = lax.dynamic_index_in_dim(picks, group, 0, keepdims=False).astype(jnp.float32)
    bias_table = up_bias.reshape(blocks, BW).astype(jnp.float32)
    bias_slots = jnp.sum(mine[:, :, None] * bias_table[None, :, :], axis=1)
    gate_slots = jnp.sum(gates[:, None, :] * mine[None, :, :], axis=2)
    up_local = up_weight.reshape(slice_rows, blocks, BW)
    down_local = down_weight.reshape(slice_rows, blocks, BW)
    paired = jnp.stack((up_local, down_local), 0)
    outgoing = jnp.einsum(
        "gsj,pdjc->gspdc", picks, paired, preferred_element_type=jnp.float32
    ).astype(jnp.bfloat16)
    received = lax.all_to_all(
        outgoing[:, :, :, None], ("row", "sub"), split_axis=0, concat_axis=3, tiled=True
    )
    weights_in = received.reshape(CAP, 2, slice_rows * group_count, BW)
    pre = jnp.einsum("rd,sdc->rsc", normed, weights_in[:, 0], preferred_element_type=jnp.float32)
    hidden = (jax.nn.relu(pre + bias_slots[None]) * gate_slots[:, :, None]).astype(jnp.bfloat16)
    partial_value = jnp.einsum(
        "rsc,sdc->rd", hidden, weights_in[:, 1], preferred_element_type=jnp.float32
    )
    summed = lax.psum_scatter(
        partial_value.astype(jnp.bfloat16), "neuron", scatter_dimension=1, tiled=True
    ).astype(jnp.float32)
    return (features.astype(jnp.float32) + summed).astype(jnp.bfloat16)

N = 4
PARTS = ((0, 32), (32, 32), (64, 32), (96, 16))
MESH = pl.DeviceIdType.MESH


def layer_kernel(
    active, counts, x_ref, gain_in, bias_in, pout_in, up_hbm, down_hbm, pin_hbm, out_ref,
    zbuf, zgain, xin, stats, terms, term_out, pre_out, pre_in, hid, outp, pbuf, rup, rdn,
    up_v, down_v, pin_v, gain_ref, bias_v, pick_v, pout_v, total_v, square_v,
    z_ss, z_rs, g_ss, g_rs, x_ss, x_rs, s_ss, s_rs, t_ss, t_rs, p_ss, p_rs, h_ss, h_rs,
    o_ss, o_rs, u_ss, u_rs, d_ss, d_rs, w_sem,
):
    n = lax.axis_index("neuron")
    row, sub = lax.axis_index("row"), lax.axis_index("sub")
    g = row * 2 + sub
    slice_w = x_ref.shape[1]
    full = slice_w * N
    f32, bf16 = jnp.float32, jnp.bfloat16

    def zdev(m):
        return {"neuron": m}

    def pdev(w):
        return {"row": w // 2, "sub": lax.rem(w, 2)}

    def send(src, dst, ss, rs, dev):
        return pltpu.make_async_remote_copy(
            src_ref=src, dst_ref=dst, send_sem=ss, recv_sem=rs, device_id=dev, device_id_type=MESH
        )

    blocks = up_v.shape[0]
    loads = [[pltpu.make_async_copy(pin_hbm, pin_v, w_sem.at[0, 0])]]
    for i, (a, b) in enumerate(((up_hbm, up_v), (down_hbm, down_v))):
        loads.append(
            [
                pltpu.make_async_copy(a.at[:, pl.ds(j * BW, BW)], b.at[j], w_sem.at[1 + i, j])
                for j in range(blocks)
            ]
        )
    zpeer = [lax.rem(n + k, N) for k in range(N)]

    def plane(k):
        flip_row, flip_sub = 1 - k // 3, lax.rem(k // 2, 2)
        return 2 * (row + flip_row - 2 * row * flip_row) + sub + flip_sub - 2 * sub * flip_sub

    ppeer = [g] + [plane(jnp.int32(k)) for k in range(1, N)]
    barrier = pltpu.get_barrier_semaphore()
    for k in range(1, N):
        pl.semaphore_signal(barrier, inc=1, device_id=zdev(zpeer[k]), device_id_type=MESH)
        pl.semaphore_signal(barrier, inc=1, device_id=pdev(ppeer[k]), device_id_type=MESH)
    pl.semaphore_wait(barrier, 2 * (N - 1))

    gain_ref[...] = gain_in[...].astype(f32)
    sent = []

    def go(copy):
        copy.start()
        sent.append(copy)

    def rows(c):
        return pl.ds(PARTS[c][0], PARTS[c][1])

    chunks = range(len(PARTS))
    def hop(m, c, up, src):
        return send(
            src, zbuf.at[m, rows(c)], z_ss.at[m, c, 0 if up else 1], z_rs.at[m, c], zdev(n + 1 if up else n - 1)
        )

    def guarded(cond, fn):
        pl.when(cond)(fn)

    for c in chunks:
        guarded(n < N - 1, lambda c=c: hop(n, c, True, x_ref.at[rows(c)]).start())
        guarded(n > 0, lambda c=c: hop(n, c, False, x_ref.at[rows(c)]).start())
    for k in range(1, N):
        go(send(gain_ref, zgain.at[n], g_ss.at[k], g_rs.at[n], zdev(zpeer[k])))
    for group in loads:
        for load in group:
            load.start()
    zbuf[n] = x_ref[...]
    zgain[n] = gain_ref[...]
    values = x_ref[...].astype(f32)
    total_v[...] = jnp.sum(values, axis=1, keepdims=True)
    square_v[...] = jnp.sum(values * values, axis=1, keepdims=True)
    place = lax.broadcasted_iota(jnp.int32, (1, 128), 1)
    for j in range(blocks):
        bias_v[j] = bias_in[:, j * BW : (j + 1) * BW].astype(f32)
        pick_v[j] = jnp.where(place == n * blocks + j, 1.0, 0.0).astype(f32)
    pick_v[blocks] = jnp.zeros((1, 128), f32)
    pout_v[...] = jnp.zeros(pout_v.shape, bf16)
    pout_v[:, : pout_in.shape[1]] = pout_in[...]

    def inward(m, c, src):
        return send(src, xin.at[g, rows(c)], x_ss.at[m, c], x_rs.at[g, c], pdev(m))

    for c in chunks:
        guarded(n != g, lambda c=c: inward(n, c, x_ref.at[rows(c)]).start())
    for far in range(1, N):
        for c in chunks:
            for up in (True, False):
                m = n - far if up else n + far

                def arrive(m=m, c=c, up=up):
                    block = zbuf.at[m, rows(c)]
                    send(x_ref.at[rows(c)], block, z_ss.at[m, c, 0], z_rs.at[m, c], zdev(zpeer[1])).wait_recv()
                    guarded(n < N - 1 if up else n > 0, lambda: hop(m, c, up, block).start())
                    guarded(m != g, lambda: inward(m, c, block).start())
                    v = zbuf[m, rows(c)].astype(f32)
                    total_v[rows(c)] += jnp.sum(v, axis=1, keepdims=True)
                    square_v[rows(c)] += jnp.sum(v * v, axis=1, keepdims=True)

                guarded(m >= 0 if up else m < N, arrive)
    for k in range(1, N):
        m = zpeer[k]
        send(gain_ref, zgain.at[m], g_ss.at[1], g_rs.at[m], zdev(m)).wait_recv()

    total, square = total_v[...], square_v[...]
    mean = total / full
    scale = lax.rsqrt(square / full - mean * mean + epsilon)
    lane = lax.broadcasted_iota(jnp.int32, (x_ref.shape[0], 128), 1)
    stats[g] = jnp.where(lane < 64, mean, scale)
    for k in range(1, N):
        go(send(stats.at[g], stats.at[g], s_ss.at[k], s_rs.at[g], pdev(ppeer[k])))

    def norm(values, mu, sc, gain):
        return ((values.astype(f32) - mu) * sc * gain).astype(bf16)

    for load in loads[0]:
        load.wait()

    def add_factor(m, acc):
        block = pin_v[pl.ds(pl.multiple_of(m * slice_w, 128), slice_w), :]
        return acc + jnp.dot(norm(zbuf[m], mean, scale, zgain[m]), block, preferred_element_type=f32)

    factor = lax.fori_loop(0, N, add_factor, jnp.zeros((x_ref.shape[0], pin_v.shape[1]), f32))
    term_out[...] = jnp.dot(factor.astype(bf16), pout_v[...], preferred_element_type=f32).astype(bf16)
    terms[n] = term_out[...]
    for k in range(1, N):
        go(send(term_out, terms.at[n], t_ss.at[k], t_rs.at[n], zdev(zpeer[k])))

    def chosen(q):
        low, high = jnp.int32(blocks), jnp.int32(-1)
        for k in range(active.shape[1]):
            local = active[q, k] - n * blocks
            inside = (k < counts[q]) & (local >= 0) & (local < blocks)
            low = jnp.minimum(low, jnp.where(inside, local, blocks))
            high = jnp.maximum(high, jnp.where(inside, local, -1))
        return low, jnp.where(high > low, high, blocks)

    def picked(ref, q):
        return jnp.concatenate([ref[jnp.minimum(i, blocks - 1)] for i in chosen(q)], axis=1)

    for load in loads[1]:
        load.wait()
    xin[g] = zbuf[g]

    def up(k, _):
        q = plane(k)

        @pl.when(k < N)
        def _():
            for c in chunks:
                send(x_ref.at[rows(c)], xin.at[q, rows(c)], x_ss.at[1, c], x_rs.at[q, c], pdev(q)).wait_recv()
            send(stats.at[g], stats.at[q], s_ss.at[1], s_rs.at[q], pdev(q)).wait_recv()

        st = stats[q]
        normed = norm(xin[q], st[:, 0:1], st[:, 64:65], zgain[g])
        pre = jnp.dot(normed, picked(up_v, q), preferred_element_type=f32)
        pre_out[q] = pre.astype(bf16)

        @pl.when(k < N)
        def _():
            send(pre_out.at[q], pre_in.at[g], p_ss.at[lax.rem(k, N)], p_rs.at[g], pdev(q)).start()

        return 0

    lax.fori_loop(1, N + 1, up, 0)
    for k in range(1, N):
        sent.append(send(pre_out.at[ppeer[k]], pre_in.at[g], p_ss.at[k], p_rs.at[g], pdev(ppeer[k])))

    for k in range(1, N):
        m = zpeer[k]
        send(term_out, terms.at[m], t_ss.at[1], t_rs.at[m], zdev(m)).wait_recv()
    scores = jnp.zeros((x_ref.shape[0], 128), f32)
    for m in range(N):
        scores = scores + terms[m].astype(f32)
    gates = jax.nn.sigmoid(scores)
    mine = chosen(g)
    gate = [jnp.sum(gates * pick_v[i], axis=1, keepdims=True) for i in mine]
    bias = [bias_v[jnp.minimum(i, blocks - 1)] for i in mine]
    pre = pre_out[g].astype(f32)
    for k in range(1, N):
        q = ppeer[k]
        send(pre_out.at[g], pre_in.at[q], p_ss.at[1], p_rs.at[q], pdev(q)).wait_recv()
        pre = pre + pre_in[q].astype(f32)
    hidden = [
        (jnp.maximum(pre[:, j * BW : (j + 1) * BW] + bias[j], 0.0) * gate[j]).astype(bf16)
        for j in range(2)
    ]
    hid[g] = jnp.concatenate(hidden, axis=1)
    for k in range(1, N):
        go(send(hid.at[g], hid.at[g], h_ss.at[k], h_rs.at[g], pdev(ppeer[k])))

    for load in loads[2]:
        load.wait()

    def down(k, _):
        q = plane(k)

        @pl.when(k < N)
        def _():
            send(hid.at[g], hid.at[q], h_ss.at[1], h_rs.at[q], pdev(q)).wait_recv()

        outp[q] = lax.dot_general(
            hid[q], picked(down_v, q), (((1,), (1,)), ((), ())), preferred_element_type=f32
        ).astype(bf16)
        return 0

    def outward(k, c):
        q = ppeer[k]
        return send(outp.at[q, rows(c)], pbuf.at[g, rows(c)], o_ss.at[k, c], o_rs.at[g, c], pdev(q))

    lax.fori_loop(1, 3, down, 0)
    for c in chunks:
        for k in (1, 2):
            go(outward(k, c))
    lax.fori_loop(3, N + 1, down, 0)
    for c in chunks:
        go(outward(3, c))
    pbuf[g] = outp[g]

    def rise(m, c, up):
        at = pbuf.at[m, rows(c)]
        if up:
            return send(at, rup.at[m, rows(c)], u_ss.at[m, c], u_rs.at[m, c], zdev(n + 1))
        return send(at, rdn.at[m, rows(c)], d_ss.at[m, c], d_rs.at[m, c], zdev(n - 1))

    def landed(m, c, up):
        buf, sems = (rup, u_rs) if up else (rdn, d_rs)
        send(x_ref.at[rows(c)], buf.at[m, rows(c)], u_ss.at[m, c], sems.at[m, c], zdev(zpeer[1])).wait_recv()

    def own(m, c):
        def wait():
            send(outp.at[0, rows(c)], pbuf.at[m, rows(c)], o_ss.at[1, c], o_rs.at[m, c], pdev(ppeer[1])).wait_recv()

        guarded(m != g, wait)

    for c in chunks:
        for far in (3, 2, 1):
            for up in (True, False):
                m = n + far if up else n - far

                def forward(m=m, c=c, up=up):
                    own(m, c)

                    def add():
                        landed(m, c, up)
                        other = rup if up else rdn
                        pbuf[m, rows(c)] = (
                            pbuf[m, rows(c)].astype(f32) + other[m, rows(c)].astype(f32)
                        ).astype(bf16)

                    guarded(n > 0 if up else n < N - 1, add)
                    rise(m, c, up).start()

                guarded(m < N if up else m >= 0, forward)
    for c in chunks:
        own(n, c)

        def middle(c=c):
            landed(n, c, True)
            landed(n, c, False)
            total = rup[n, rows(c)].astype(f32) + rdn[n, rows(c)].astype(f32) + pbuf[n, rows(c)].astype(f32)
            out_ref[rows(c)] = (x_ref[rows(c)].astype(f32) + total).astype(bf16)

        def edge(c=c, up=True):
            landed(n, c, up)
            other = rup if up else rdn
            total = other[n, rows(c)].astype(f32) + pbuf[n, rows(c)].astype(f32)
            out_ref[rows(c)] = (x_ref[rows(c)].astype(f32) + total).astype(bf16)

        guarded(n == 0, lambda c=c: edge(c, False))
        guarded(n == N - 1, lambda c=c: edge(c, True))
        guarded((n > 0) & (n < N - 1), middle)
    for c in chunks:
        for m in range(N):
            guarded((n >= m) & (n < N - 1), lambda m=m, c=c: hop(m, c, True, x_ref.at[rows(c)]).wait_send())
            guarded((n <= m) & (n > 0), lambda m=m, c=c: hop(m, c, False, x_ref.at[rows(c)]).wait_send())
            guarded(g != m, lambda m=m, c=c: inward(m, c, x_ref.at[rows(c)]).wait_send())
            guarded(n < m, lambda m=m, c=c: rise(m, c, True).wait_send())
            guarded(n > m, lambda m=m, c=c: rise(m, c, False).wait_send())
    for copy in sent:
        copy.wait_send()


def fused_device(
    features, ln_gain, up_weight, up_bias, down_weight, pred_in, pred_out, active, counts
):
    blocks = up_weight.shape[1] // BW
    height, slice_w = features.shape
    vmem = pl.BlockSpec(memory_space=pltpu.VMEM)
    hbm = pl.BlockSpec(memory_space=pl.ANY)
    nc = len(PARTS)
    bf16, f32 = jnp.bfloat16, jnp.float32
    dma = pltpu.SemaphoreType.DMA
    return pl.pallas_call(
        layer_kernel,
        out_shape=jax.ShapeDtypeStruct(features.shape, bf16),
        in_specs=[pl.BlockSpec(memory_space=pltpu.SMEM)] * 2 + [vmem] * 4 + [hbm] * 3,
        out_specs=vmem,
        scratch_shapes=[
            pltpu.VMEM((N, height, slice_w), bf16),
            pltpu.VMEM((N, 1, slice_w), f32),
            pltpu.VMEM((N, height, slice_w), bf16),
            pltpu.VMEM((N, height, 128), f32),
            pltpu.VMEM((N, height, 128), bf16),
            pltpu.VMEM((height, 128), bf16),
            pltpu.VMEM((N, height, CAP * BW), bf16),
            pltpu.VMEM((N, height, CAP * BW), bf16),
            pltpu.VMEM((N, height, CAP * BW), bf16),
            pltpu.VMEM((N, height, slice_w), bf16),
            pltpu.VMEM((N, height, slice_w), bf16),
            pltpu.VMEM((N, height, slice_w), bf16),
            pltpu.VMEM((N, height, slice_w), bf16),
            pltpu.VMEM((blocks, up_weight.shape[0], BW), bf16),
            pltpu.VMEM((blocks, down_weight.shape[0], BW), bf16),
            pltpu.VMEM(pred_in.shape, bf16),
            pltpu.VMEM((1, slice_w), f32),
            pltpu.VMEM((blocks, 1, BW), f32),
            pltpu.VMEM((blocks + 1, 1, 128), f32),
            pltpu.VMEM((pred_out.shape[0], 128), bf16),
            pltpu.VMEM((height, 1), f32),
            pltpu.VMEM((height, 1), f32),
            dma((N, nc, 2)), dma((N, nc)),
            dma((N,)), dma((N,)),
            dma((N, nc)), dma((N, nc)),
            dma((N,)), dma((N,)),
            dma((N,)), dma((N,)),
            dma((N,)), dma((N,)),
            dma((N,)), dma((N,)),
            dma((N, nc)), dma((N, nc)),
            dma((N, nc)), dma((N, nc)),
            dma((N, nc)), dma((N, nc)),
            dma((3, blocks)),
        ],
        compiler_params=pltpu.CompilerParams(
            collective_id=0, has_side_effects=True, vmem_limit_bytes=50 * 1024 * 1024
        ),
    )(
        active, counts, features, ln_gain.reshape(1, -1), up_bias.reshape(1, -1), pred_out,
        up_weight, down_weight, pred_in,
    )


def solution(mesh):
    placed = (
        P(("groups", "row", "sub"), "neuron"),
        P("neuron"),
        P(("row", "sub"), "neuron"),
        P("neuron"),
        P(("row", "sub"), "neuron"),
        P(None, "neuron"),
        P("neuron", None),
        P("groups", None),
        P("groups"),
    )
    small = mesh.shape["neuron"] == N and mesh.shape["row"] == 2 and mesh.shape["sub"] == 2
    return jax.shard_map(
        fused_device if small else per_device,
        mesh=mesh,
        in_specs=placed,
        out_specs=P(("groups", "row", "sub"), "neuron"),
        check_vma=False,
    )
```

```python
import jax
import jax.numpy as jnp
from jax import lax
from jax.experimental import pallas as pl
from jax.experimental.pallas import tpu as pltpu
from jax.sharding import PartitionSpec as P

BW = 128
CAP = 2


epsilon = 1e-05


def normalize(values, gain, width_all, total, square):
    mean = total / width_all
    spread = square / width_all - mean * mean
    return ((values - mean) * lax.rsqrt(spread + epsilon) * gain.astype(jnp.float32)).astype(
        jnp.bfloat16
    )


def per_device(
    features, ln_gain, up_weight, up_bias, down_weight, pred_in, pred_out, active, counts
):
    group_count = lax.axis_size(("row", "sub"))
    neuron = lax.axis_index("neuron")
    group = lax.axis_index(("row", "sub"))
    slice_rows = up_weight.shape[0]
    blocks = up_weight.shape[1] // BW
    whole, gain_all = (
        lax.all_gather(features, "neuron", axis=1, tiled=True),
        lax.all_gather(ln_gain, "neuron", axis=0, tiled=True),
    )
    values = whole.astype(jnp.float32)
    normed = normalize(
        values,
        gain_all,
        values.shape[1],
        jnp.sum(values, axis=1, keepdims=True),
        jnp.sum(values * values, axis=1, keepdims=True),
    )
    factor = jnp.dot(normed, pred_in, preferred_element_type=jnp.float32).astype(jnp.bfloat16)
    terms = jnp.dot(factor, pred_out, preferred_element_type=jnp.float32)
    scores = lax.psum_scatter(
        terms.astype(jnp.bfloat16), "neuron", scatter_dimension=1, tiled=True
    ).astype(jnp.float32)
    gates = jax.nn.sigmoid(scores)
    live = lax.broadcasted_iota(jnp.int32, active.shape, 1) < counts[:, None]
    local_ids = neuron * blocks + jnp.arange(blocks, dtype=jnp.int32)
    chosen = jnp.any(
        (active[:, :, None] == local_ids[None, None, :]) & live[:, :, None], axis=1
    ).astype(jnp.int32)
    order = jnp.cumsum(chosen, axis=1) - 1
    slots = jnp.arange(CAP, dtype=jnp.int32)
    picks = ((order[:, None, :] == slots[None, :, None]) & (chosen[:, None, :] == 1)).astype(
        jnp.bfloat16
    )
    mine = lax.dynamic_index_in_dim(picks, group, 0, keepdims=False).astype(jnp.float32)
    bias_table = up_bias.reshape(blocks, BW).astype(jnp.float32)
    bias_slots = jnp.sum(mine[:, :, None] * bias_table[None, :, :], axis=1)
    gate_slots = jnp.sum(gates[:, None, :] * mine[None, :, :], axis=2)
    up_local = up_weight.reshape(slice_rows, blocks, BW)
    down_local = down_weight.reshape(slice_rows, blocks, BW)
    paired = jnp.stack((up_local, down_local), 0)
    outgoing = jnp.einsum(
        "gsj,pdjc->gspdc", picks, paired, preferred_element_type=jnp.float32
    ).astype(jnp.bfloat16)
    received = lax.all_to_all(
        outgoing[:, :, :, None], ("row", "sub"), split_axis=0, concat_axis=3, tiled=True
    )
    weights_in = received.reshape(CAP, 2, slice_rows * group_count, BW)
    pre = jnp.einsum("rd,sdc->rsc", normed, weights_in[:, 0], preferred_element_type=jnp.float32)
    hidden = (jax.nn.relu(pre + bias_slots[None]) * gate_slots[:, :, None]).astype(jnp.bfloat16)
    partial_value = jnp.einsum(
        "rsc,sdc->rd", hidden, weights_in[:, 1], preferred_element_type=jnp.float32
    )
    summed = lax.psum_scatter(
        partial_value.astype(jnp.bfloat16), "neuron", scatter_dimension=1, tiled=True
    ).astype(jnp.float32)
    return (features.astype(jnp.float32) + summed).astype(jnp.bfloat16)

N = 4
PARTS = ((0, 32), (32, 32), (64, 32), (96, 16))
HALVES = ((0, 64, (0, 1)), (64, 48, (2, 3)))
MESH = pl.DeviceIdType.MESH


def layer_kernel(
    active, counts, x_ref, gain_in, bias_in, pout_in, up_hbm, down_hbm, pin_hbm, out_ref,
    zbuf, zgain, xin, stats, terms, term_out, pre_out, pre_in, hid, outp, pbuf, rup, rdn,
    up_v, down_v, pin_v, gain_ref, bias_v, pick_v, pout_v, total_v, square_v,
    z_ss, z_rs, g_ss, g_rs, x_ss, x_rs, s_ss, s_rs, t_ss, t_rs, p_ss, p_rs, h_ss, h_rs,
    o_ss, o_rs, u_ss, u_rs, d_ss, d_rs, w_sem,
):
    n = lax.axis_index("neuron")
    row, sub = lax.axis_index("row"), lax.axis_index("sub")
    g = row * 2 + sub
    slice_w = x_ref.shape[1]
    full = slice_w * N
    f32, bf16 = jnp.float32, jnp.bfloat16

    def zdev(m):
        return {"neuron": m}

    def pdev(w):
        return {"row": w // 2, "sub": lax.rem(w, 2)}

    def send(src, dst, ss, rs, dev):
        return pltpu.make_async_remote_copy(
            src_ref=src, dst_ref=dst, send_sem=ss, recv_sem=rs, device_id=dev, device_id_type=MESH
        )

    blocks = up_v.shape[0]
    loads = [[pltpu.make_async_copy(pin_hbm, pin_v, w_sem.at[0, 0])]]
    for i, (a, b) in enumerate(((up_hbm, up_v), (down_hbm, down_v))):
        loads.append(
            [
                pltpu.make_async_copy(a.at[:, pl.ds(j * BW, BW)], b.at[j], w_sem.at[1 + i, j])
                for j in range(blocks)
            ]
        )
    zpeer = [lax.rem(n + k, N) for k in range(N)]

    def plane(k):
        flip_row, flip_sub = 1 - k // 3, lax.rem(k // 2, 2)
        return 2 * (row + flip_row - 2 * row * flip_row) + sub + flip_sub - 2 * sub * flip_sub

    ppeer = [g] + [plane(jnp.int32(k)) for k in range(1, N)]
    barrier = pltpu.get_barrier_semaphore()
    for k in range(1, N):
        pl.semaphore_signal(barrier, inc=1, device_id=zdev(zpeer[k]), device_id_type=MESH)
        pl.semaphore_signal(barrier, inc=1, device_id=pdev(ppeer[k]), device_id_type=MESH)
    pl.semaphore_wait(barrier, 2 * (N - 1))

    gain_ref[...] = gain_in[...].astype(f32)
    sent = []

    def go(copy):
        copy.start()
        sent.append(copy)

    def rows(c):
        return pl.ds(PARTS[c][0], PARTS[c][1])

    chunks = range(len(PARTS))
    def hop(m, c, up, src):
        return send(
            src, zbuf.at[m, rows(c)], z_ss.at[m, c, 0 if up else 1], z_rs.at[m, c], zdev(n + 1 if up else n - 1)
        )

    def guarded(cond, fn):
        pl.when(cond)(fn)

    for c in chunks:
        guarded(n < N - 1, lambda c=c: hop(n, c, True, x_ref.at[rows(c)]).start())
        guarded(n > 0, lambda c=c: hop(n, c, False, x_ref.at[rows(c)]).start())
    for k in range(1, N):
        go(send(gain_ref, zgain.at[n], g_ss.at[k], g_rs.at[n], zdev(zpeer[k])))
    for group in loads:
        for load in group:
            load.start()
    zbuf[n] = x_ref[...]
    zgain[n] = gain_ref[...]
    values = x_ref[...].astype(f32)
    total_v[...] = jnp.sum(values, axis=1, keepdims=True)
    square_v[...] = jnp.sum(values * values, axis=1, keepdims=True)
    place = lax.broadcasted_iota(jnp.int32, (1, 128), 1)
    for j in range(blocks):
        bias_v[j] = bias_in[:, j * BW : (j + 1) * BW].astype(f32)
        pick_v[j] = jnp.where(place == n * blocks + j, 1.0, 0.0).astype(f32)
    pick_v[blocks] = jnp.zeros((1, 128), f32)
    pout_v[...] = jnp.zeros(pout_v.shape, bf16)
    pout_v[:, : pout_in.shape[1]] = pout_in[...]

    def inward(m, c, src):
        return send(src, xin.at[g, rows(c)], x_ss.at[m, c], x_rs.at[g, c], pdev(m))

    for c in chunks:
        guarded(n != g, lambda c=c: inward(n, c, x_ref.at[rows(c)]).start())
    def arrivals(far, h):
        for c in HALVES[h][2]:
            for up in (True, False):
                m = n - far if up else n + far

                def arrive(m=m, c=c, up=up):
                    block = zbuf.at[m, rows(c)]
                    send(x_ref.at[rows(c)], block, z_ss.at[m, c, 0], z_rs.at[m, c], zdev(zpeer[1])).wait_recv()
                    guarded(n < N - 1 if up else n > 0, lambda: hop(m, c, up, block).start())
                    guarded(m != g, lambda: inward(m, c, block).start())
                    v = zbuf[m, rows(c)].astype(f32)
                    total_v[rows(c)] += jnp.sum(v, axis=1, keepdims=True)
                    square_v[rows(c)] += jnp.sum(v * v, axis=1, keepdims=True)

                guarded(m >= 0 if up else m < N, arrive)
    def wait_loads(i):
        for load in loads[i]:
            load.wait()

    def half(h):
        return pl.ds(HALVES[h][0], HALVES[h][1])

    def norm(values, mu, sc, gain):
        return ((values.astype(f32) - mu) * sc * gain).astype(bf16)

    def chosen(q):
        low, high = jnp.int32(blocks), jnp.int32(-1)
        for k in range(active.shape[1]):
            local = active[q, k] - n * blocks
            inside = (k < counts[q]) & (local >= 0) & (local < blocks)
            low = jnp.minimum(low, jnp.where(inside, local, blocks))
            high = jnp.maximum(high, jnp.where(inside, local, -1))
        return low, jnp.where(high > low, high, blocks)

    def picked(ref, q):
        return jnp.concatenate([ref[jnp.minimum(i, blocks - 1)] for i in chosen(q)], axis=1)

    def stats_of(h):
        at = half(h)
        mean = total_v[at] / full
        scale = lax.rsqrt(square_v[at] / full - mean * mean + epsilon)
        lane = lax.broadcasted_iota(jnp.int32, (HALVES[h][1], 128), 1)
        stats[g, at] = jnp.where(lane < 64, mean, scale)
        xin[g, at] = zbuf[g, at]
        for k in range(1, N):
            go(send(stats.at[g, at], stats.at[g, at], s_ss.at[k, h], s_rs.at[g, h], pdev(ppeer[k])))

    def factors(h):
        at = half(h)
        st = stats[g, at]

        def add_factor(m, acc):
            block = pin_v[pl.ds(pl.multiple_of(m * slice_w, 128), slice_w), :]
            normed = norm(zbuf[m, at], st[:, 0:1], st[:, 64:65], zgain[m])
            return acc + jnp.dot(normed, block, preferred_element_type=f32)

        factor = lax.fori_loop(0, N, add_factor, jnp.zeros((HALVES[h][1], pin_v.shape[1]), f32))
        term_out[at] = jnp.dot(factor.astype(bf16), pout_v[...], preferred_element_type=f32).astype(bf16)
        terms[n, at] = term_out[at]
        for k in range(1, N):
            go(send(term_out.at[at], terms.at[n, at], t_ss.at[k, h], t_rs.at[n, h], zdev(zpeer[k])))

    def pre_send(k, q, h):
        at = half(h)
        return send(pre_out.at[q, at], pre_in.at[g, at], p_ss.at[lax.rem(k, N), h], p_rs.at[g, h], pdev(q))

    def ups(h):
        at = half(h)

        def up(k, _):
            q = plane(k)

            @pl.when(k < N)
            def _():
                for c in HALVES[h][2]:
                    send(x_ref.at[rows(c)], xin.at[q, rows(c)], x_ss.at[1, c], x_rs.at[q, c], pdev(q)).wait_recv()
                send(stats.at[g, at], stats.at[q, at], s_ss.at[1, h], s_rs.at[q, h], pdev(q)).wait_recv()

            st = stats[q, at]
            normed = norm(xin[q, at], st[:, 0:1], st[:, 64:65], zgain[g])
            pre_out[q, at] = jnp.dot(normed, picked(up_v, q), preferred_element_type=f32).astype(bf16)

            @pl.when(k < N)
            def _():
                pre_send(k, q, h).start()

            return 0

        lax.fori_loop(1, N + 1, up, 0)
        for k in range(1, N):
            sent.append(pre_send(jnp.int32(k), ppeer[k], h))

    def hiddens(h):
        at = half(h)
        for k in range(1, N):
            m = zpeer[k]
            send(term_out.at[at], terms.at[m, at], t_ss.at[1, h], t_rs.at[m, h], zdev(m)).wait_recv()
        scores = jnp.zeros((HALVES[h][1], 128), f32)
        for m in range(N):
            scores = scores + terms[m, at].astype(f32)
        gates = jax.nn.sigmoid(scores)
        mine = chosen(g)
        gate = [jnp.sum(gates * pick_v[i], axis=1, keepdims=True) for i in mine]
        bias = [bias_v[jnp.minimum(i, blocks - 1)] for i in mine]
        pre = pre_out[g, at].astype(f32)
        for k in range(1, N):
            q = ppeer[k]
            send(pre_out.at[g, at], pre_in.at[q, at], p_ss.at[1, h], p_rs.at[q, h], pdev(q)).wait_recv()
            pre = pre + pre_in[q, at].astype(f32)
        hidden = [
            (jnp.maximum(pre[:, j * BW : (j + 1) * BW] + bias[j], 0.0) * gate[j]).astype(bf16)
            for j in range(2)
        ]
        hid[g, at] = jnp.concatenate(hidden, axis=1)
        for k in range(1, N):
            go(send(hid.at[g, at], hid.at[g, at], h_ss.at[k, h], h_rs.at[g, h], pdev(ppeer[k])))

    def outward(k, c):
        q = ppeer[k]
        return send(outp.at[q, rows(c)], pbuf.at[g, rows(c)], o_ss.at[k, c], o_rs.at[g, c], pdev(q))

    def downs(h):
        at = half(h)

        def down(k, _):
            q = plane(k)

            @pl.when(k < N)
            def _():
                send(hid.at[g, at], hid.at[q, at], h_ss.at[1, h], h_rs.at[q, h], pdev(q)).wait_recv()

            outp[q, at] = lax.dot_general(
                hid[q, at], picked(down_v, q), (((1,), (1,)), ((), ())), preferred_element_type=f32
            ).astype(bf16)
            return 0

        lax.fori_loop(1, 3, down, 0)
        for c in HALVES[h][2]:
            for k in (1, 2):
                go(outward(k, c))
        lax.fori_loop(3, N + 1, down, 0)
        for c in HALVES[h][2]:
            go(outward(3, c))
        pbuf[g, at] = outp[g, at]

    def rise(m, c, up):
        at = pbuf.at[m, rows(c)]
        if up:
            return send(at, rup.at[m, rows(c)], u_ss.at[m, c], u_rs.at[m, c], zdev(n + 1))
        return send(at, rdn.at[m, rows(c)], d_ss.at[m, c], d_rs.at[m, c], zdev(n - 1))

    def landed(m, c, up):
        buf, sems = (rup, u_rs) if up else (rdn, d_rs)
        send(x_ref.at[rows(c)], buf.at[m, rows(c)], u_ss.at[m, c], sems.at[m, c], zdev(zpeer[1])).wait_recv()

    def own(m, c):
        def wait():
            send(outp.at[0, rows(c)], pbuf.at[m, rows(c)], o_ss.at[1, c], o_rs.at[m, c], pdev(ppeer[1])).wait_recv()

        guarded(m != g, wait)

    def rises(far, h):
        for c in HALVES[h][2]:
            for up in (True, False):
                m = n + far if up else n - far

                def forward(m=m, c=c, up=up):
                    own(m, c)

                    def add():
                        landed(m, c, up)
                        other = rup if up else rdn
                        pbuf[m, rows(c)] = (
                            pbuf[m, rows(c)].astype(f32) + other[m, rows(c)].astype(f32)
                        ).astype(bf16)

                    guarded(n > 0 if up else n < N - 1, add)
                    rise(m, c, up).start()

                guarded(m < N if up else m >= 0, forward)
    for far in range(1, N):
        arrivals(far, 0)
    for k in range(1, N):
        m = zpeer[k]
        send(gain_ref, zgain.at[m], g_ss.at[1], g_rs.at[m], zdev(m)).wait_recv()

    stats_of(0)
    wait_loads(0)
    arrivals(1, 1)
    factors(0)
    wait_loads(1)
    ups(0)
    arrivals(2, 1)
    hiddens(0)
    wait_loads(2)
    arrivals(3, 1)
    stats_of(1)
    downs(0)
    factors(1)
    rises(3, 0)
    ups(1)
    rises(2, 0)
    hiddens(1)
    rises(1, 0)
    downs(1)
    for far in (3, 2, 1):
        rises(far, 1)
    for c in chunks:
        own(n, c)

        def middle(c=c):
            landed(n, c, True)
            landed(n, c, False)
            total = rup[n, rows(c)].astype(f32) + rdn[n, rows(c)].astype(f32) + pbuf[n, rows(c)].astype(f32)
            out_ref[rows(c)] = (x_ref[rows(c)].astype(f32) + total).astype(bf16)

        def edge(c=c, up=True):
            landed(n, c, up)
            other = rup if up else rdn
            total = other[n, rows(c)].astype(f32) + pbuf[n, rows(c)].astype(f32)
            out_ref[rows(c)] = (x_ref[rows(c)].astype(f32) + total).astype(bf16)

        guarded(n == 0, lambda c=c: edge(c, False))
        guarded(n == N - 1, lambda c=c: edge(c, True))
        guarded((n > 0) & (n < N - 1), middle)
    for c in chunks:
        for m in range(N):
            guarded((n >= m) & (n < N - 1), lambda m=m, c=c: hop(m, c, True, x_ref.at[rows(c)]).wait_send())
            guarded((n <= m) & (n > 0), lambda m=m, c=c: hop(m, c, False, x_ref.at[rows(c)]).wait_send())
            guarded(g != m, lambda m=m, c=c: inward(m, c, x_ref.at[rows(c)]).wait_send())
            guarded(n < m, lambda m=m, c=c: rise(m, c, True).wait_send())
            guarded(n > m, lambda m=m, c=c: rise(m, c, False).wait_send())
    for copy in sent:
        copy.wait_send()


def fused_device(
    features, ln_gain, up_weight, up_bias, down_weight, pred_in, pred_out, active, counts
):
    blocks = up_weight.shape[1] // BW
    height, slice_w = features.shape
    vmem = pl.BlockSpec(memory_space=pltpu.VMEM)
    hbm = pl.BlockSpec(memory_space=pl.ANY)
    nc = len(PARTS)
    bf16, f32 = jnp.bfloat16, jnp.float32
    dma = pltpu.SemaphoreType.DMA
    return pl.pallas_call(
        layer_kernel,
        out_shape=jax.ShapeDtypeStruct(features.shape, bf16),
        in_specs=[pl.BlockSpec(memory_space=pltpu.SMEM)] * 2 + [vmem] * 4 + [hbm] * 3,
        out_specs=vmem,
        scratch_shapes=[
            pltpu.VMEM((N, height, slice_w), bf16),
            pltpu.VMEM((N, 1, slice_w), f32),
            pltpu.VMEM((N, height, slice_w), bf16),
            pltpu.VMEM((N, height, 128), f32),
            pltpu.VMEM((N, height, 128), bf16),
            pltpu.VMEM((height, 128), bf16),
            pltpu.VMEM((N, height, CAP * BW), bf16),
            pltpu.VMEM((N, height, CAP * BW), bf16),
            pltpu.VMEM((N, height, CAP * BW), bf16),
            pltpu.VMEM((N, height, slice_w), bf16),
            pltpu.VMEM((N, height, slice_w), bf16),
            pltpu.VMEM((N, height, slice_w), bf16),
            pltpu.VMEM((N, height, slice_w), bf16),
            pltpu.VMEM((blocks, up_weight.shape[0], BW), bf16),
            pltpu.VMEM((blocks, down_weight.shape[0], BW), bf16),
            pltpu.VMEM(pred_in.shape, bf16),
            pltpu.VMEM((1, slice_w), f32),
            pltpu.VMEM((blocks, 1, BW), f32),
            pltpu.VMEM((blocks + 1, 1, 128), f32),
            pltpu.VMEM((pred_out.shape[0], 128), bf16),
            pltpu.VMEM((height, 1), f32),
            pltpu.VMEM((height, 1), f32),
            dma((N, nc, 2)), dma((N, nc)),
            dma((N,)), dma((N,)),
            dma((N, nc)), dma((N, nc)),
            dma((N, 2)), dma((N, 2)),
            dma((N, 2)), dma((N, 2)),
            dma((N, 2)), dma((N, 2)),
            dma((N, 2)), dma((N, 2)),
            dma((N, nc)), dma((N, nc)),
            dma((N, nc)), dma((N, nc)),
            dma((N, nc)), dma((N, nc)),
            dma((3, blocks)),
        ],
        compiler_params=pltpu.CompilerParams(
            collective_id=0, has_side_effects=True, vmem_limit_bytes=50 * 1024 * 1024
        ),
    )(
        active, counts, features, ln_gain.reshape(1, -1), up_bias.reshape(1, -1), pred_out,
        up_weight, down_weight, pred_in,
    )


def solution(mesh):
    placed = (
        P(("groups", "row", "sub"), "neuron"),
        P("neuron"),
        P(("row", "sub"), "neuron"),
        P("neuron"),
        P(("row", "sub"), "neuron"),
        P(None, "neuron"),
        P("neuron", None),
        P("groups", None),
        P("groups"),
    )
    small = mesh.shape["neuron"] == N and mesh.shape["row"] == 2 and mesh.shape["sub"] == 2
    return jax.shard_map(
        fused_device if small else per_device,
        mesh=mesh,
        in_specs=placed,
        out_specs=P(("groups", "row", "sub"), "neuron"),
        check_vma=False,
    )
```

```python
import jax
import jax.numpy as jnp
from jax import lax
from jax.experimental import pallas as pl
from jax.experimental.pallas import tpu as pltpu
from jax.sharding import PartitionSpec as P

BW = 128
CAP = 2


epsilon = 1e-05


def normalize(values, gain, width_all, total, square):
    mean = total / width_all
    spread = square / width_all - mean * mean
    return ((values - mean) * lax.rsqrt(spread + epsilon) * gain.astype(jnp.float32)).astype(
        jnp.bfloat16
    )


def per_device(
    features, ln_gain, up_weight, up_bias, down_weight, pred_in, pred_out, active, counts
):
    group_count = lax.axis_size(("row", "sub"))
    neuron = lax.axis_index("neuron")
    group = lax.axis_index(("row", "sub"))
    slice_rows = up_weight.shape[0]
    blocks = up_weight.shape[1] // BW
    whole, gain_all = (
        lax.all_gather(features, "neuron", axis=1, tiled=True),
        lax.all_gather(ln_gain, "neuron", axis=0, tiled=True),
    )
    values = whole.astype(jnp.float32)
    normed = normalize(
        values,
        gain_all,
        values.shape[1],
        jnp.sum(values, axis=1, keepdims=True),
        jnp.sum(values * values, axis=1, keepdims=True),
    )
    factor = jnp.dot(normed, pred_in, preferred_element_type=jnp.float32).astype(jnp.bfloat16)
    terms = jnp.dot(factor, pred_out, preferred_element_type=jnp.float32)
    scores = lax.psum_scatter(
        terms.astype(jnp.bfloat16), "neuron", scatter_dimension=1, tiled=True
    ).astype(jnp.float32)
    gates = jax.nn.sigmoid(scores)
    live = lax.broadcasted_iota(jnp.int32, active.shape, 1) < counts[:, None]
    local_ids = neuron * blocks + jnp.arange(blocks, dtype=jnp.int32)
    chosen = jnp.any(
        (active[:, :, None] == local_ids[None, None, :]) & live[:, :, None], axis=1
    ).astype(jnp.int32)
    order = jnp.cumsum(chosen, axis=1) - 1
    slots = jnp.arange(CAP, dtype=jnp.int32)
    picks = ((order[:, None, :] == slots[None, :, None]) & (chosen[:, None, :] == 1)).astype(
        jnp.bfloat16
    )
    mine = lax.dynamic_index_in_dim(picks, group, 0, keepdims=False).astype(jnp.float32)
    bias_table = up_bias.reshape(blocks, BW).astype(jnp.float32)
    bias_slots = jnp.sum(mine[:, :, None] * bias_table[None, :, :], axis=1)
    gate_slots = jnp.sum(gates[:, None, :] * mine[None, :, :], axis=2)
    up_local = up_weight.reshape(slice_rows, blocks, BW)
    down_local = down_weight.reshape(slice_rows, blocks, BW)
    paired = jnp.stack((up_local, down_local), 0)
    outgoing = jnp.einsum(
        "gsj,pdjc->gspdc", picks, paired, preferred_element_type=jnp.float32
    ).astype(jnp.bfloat16)
    received = lax.all_to_all(
        outgoing[:, :, :, None], ("row", "sub"), split_axis=0, concat_axis=3, tiled=True
    )
    weights_in = received.reshape(CAP, 2, slice_rows * group_count, BW)
    pre = jnp.einsum("rd,sdc->rsc", normed, weights_in[:, 0], preferred_element_type=jnp.float32)
    hidden = (jax.nn.relu(pre + bias_slots[None]) * gate_slots[:, :, None]).astype(jnp.bfloat16)
    partial_value = jnp.einsum(
        "rsc,sdc->rd", hidden, weights_in[:, 1], preferred_element_type=jnp.float32
    )
    summed = lax.psum_scatter(
        partial_value.astype(jnp.bfloat16), "neuron", scatter_dimension=1, tiled=True
    ).astype(jnp.float32)
    return (features.astype(jnp.float32) + summed).astype(jnp.bfloat16)

N = 4
PARTS = ((0, 32), (32, 32), (64, 32), (96, 16))
HALVES = ((0, 64, (0, 1)), (64, 48, (2, 3)))
MESH = pl.DeviceIdType.MESH


def layer_kernel(
    active, counts, x_ref, vectors, pout_hbm, up_hbm, down_hbm, pin_hbm, out_ref,
    zbuf, zgain, xin, stats, terms, term_out, pre_out, pre_in, hid, outp, pbuf, rup, rdn,
    up_v, down_v, pin_v, gain_ref, bias_v, pick_v, pout_in, pout_v, total_v, square_v,
    z_ss, z_rs, g_ss, g_rs, x_ss, x_rs, s_ss, s_rs, t_ss, t_rs, p_ss, p_rs, h_ss, h_rs,
    o_ss, o_rs, u_ss, u_rs, d_ss, d_rs, w_sem,
):
    n = lax.axis_index("neuron")
    row, sub = lax.axis_index("row"), lax.axis_index("sub")
    g = row * 2 + sub
    slice_w = x_ref.shape[1]
    full = slice_w * N
    f32, bf16 = jnp.float32, jnp.bfloat16

    def zdev(m):
        return {"neuron": m}

    def pdev(w):
        return {"row": w // 2, "sub": lax.rem(w, 2)}

    def send(src, dst, ss, rs, dev):
        return pltpu.make_async_remote_copy(
            src_ref=src, dst_ref=dst, send_sem=ss, recv_sem=rs, device_id=dev, device_id_type=MESH
        )

    blocks = up_v.shape[0]
    loads = [
        [
            pltpu.make_async_copy(pin_hbm, pin_v, w_sem.at[0, 0]),
            pltpu.make_async_copy(pout_hbm, pout_in, w_sem.at[0, 1]),
        ]
    ]
    for i, (a, b) in enumerate(((up_hbm, up_v), (down_hbm, down_v))):
        loads.append(
            [
                pltpu.make_async_copy(a.at[:, pl.ds(j * BW, BW)], b.at[j], w_sem.at[1 + i, j])
                for j in range(blocks)
            ]
        )
    zpeer = [lax.rem(n + k, N) for k in range(N)]

    def plane(k):
        flip_row, flip_sub = 1 - k // 3, lax.rem(k // 2, 2)
        return 2 * (row + flip_row - 2 * row * flip_row) + sub + flip_sub - 2 * sub * flip_sub

    ppeer = [g] + [plane(jnp.int32(k)) for k in range(1, N)]
    barrier = pltpu.get_barrier_semaphore()
    for k in range(1, N):
        pl.semaphore_signal(barrier, inc=1, device_id=zdev(zpeer[k]), device_id_type=MESH)
        pl.semaphore_signal(barrier, inc=1, device_id=pdev(ppeer[k]), device_id_type=MESH)
    pl.semaphore_wait(barrier, 2 * (N - 1))

    gain_ref[...] = vectors[:, :slice_w].astype(f32)
    sent = []

    def go(copy):
        copy.start()
        sent.append(copy)

    def rows(c):
        return pl.ds(PARTS[c][0], PARTS[c][1])

    chunks = range(len(PARTS))
    def hop(m, c, up, src):
        return send(
            src, zbuf.at[m, rows(c)], z_ss.at[m, c, 0 if up else 1], z_rs.at[m, c], zdev(n + 1 if up else n - 1)
        )

    def guarded(cond, fn):
        pl.when(cond)(fn)

    for c in chunks:
        guarded(n < N - 1, lambda c=c: hop(n, c, True, x_ref.at[rows(c)]).start())
        guarded(n > 0, lambda c=c: hop(n, c, False, x_ref.at[rows(c)]).start())
    for k in range(1, N):
        go(send(gain_ref, zgain.at[n], g_ss.at[k], g_rs.at[n], zdev(zpeer[k])))
    for group in loads:
        for load in group:
            load.start()
    zbuf[n] = x_ref[...]
    zgain[n] = gain_ref[...]
    values = x_ref[...].astype(f32)
    total_v[...] = jnp.sum(values, axis=1, keepdims=True)
    square_v[...] = jnp.sum(values * values, axis=1, keepdims=True)
    place = lax.broadcasted_iota(jnp.int32, (1, 128), 1)
    for j in range(blocks):
        bias_v[j] = vectors[:, slice_w + j * BW : slice_w + (j + 1) * BW].astype(f32)
        pick_v[j] = jnp.where(place == n * blocks + j, 1.0, 0.0).astype(f32)
    pick_v[blocks] = jnp.zeros((1, 128), f32)

    def inward(m, c, src):
        return send(src, xin.at[g, rows(c)], x_ss.at[m, c], x_rs.at[g, c], pdev(m))

    for c in chunks:
        guarded(n != g, lambda c=c: inward(n, c, x_ref.at[rows(c)]).start())
    def arrivals(far, h):
        for c in HALVES[h][2]:
            for up in (True, False):
                m = n - far if up else n + far

                def arrive(m=m, c=c, up=up):
                    block = zbuf.at[m, rows(c)]
                    send(x_ref.at[rows(c)], block, z_ss.at[m, c, 0], z_rs.at[m, c], zdev(zpeer[1])).wait_recv()
                    guarded(n < N - 1 if up else n > 0, lambda: hop(m, c, up, block).start())
                    guarded(m != g, lambda: inward(m, c, block).start())
                    v = zbuf[m, rows(c)].astype(f32)
                    total_v[rows(c)] += jnp.sum(v, axis=1, keepdims=True)
                    square_v[rows(c)] += jnp.sum(v * v, axis=1, keepdims=True)

                guarded(m >= 0 if up else m < N, arrive)
    def wait_loads(i):
        for load in loads[i]:
            load.wait()

    def half(h):
        return pl.ds(HALVES[h][0], HALVES[h][1])

    def norm(values, mu, sc, gain):
        return ((values.astype(f32) - mu) * sc * gain).astype(bf16)

    def chosen(q):
        low, high = jnp.int32(blocks), jnp.int32(-1)
        for k in range(active.shape[1]):
            local = active[q, k] - n * blocks
            inside = (k < counts[q]) & (local >= 0) & (local < blocks)
            low = jnp.minimum(low, jnp.where(inside, local, blocks))
            high = jnp.maximum(high, jnp.where(inside, local, -1))
        return low, jnp.where(high > low, high, blocks)

    def picked(ref, q):
        return jnp.concatenate([ref[jnp.minimum(i, blocks - 1)] for i in chosen(q)], axis=1)

    def stats_of(h):
        at = half(h)
        mean = total_v[at] / full
        scale = lax.rsqrt(square_v[at] / full - mean * mean + epsilon)
        lane = lax.broadcasted_iota(jnp.int32, (HALVES[h][1], 128), 1)
        stats[g, at] = jnp.where(lane < 64, mean, scale)
        xin[g, at] = zbuf[g, at]
        for k in range(1, N):
            go(send(stats.at[g, at], stats.at[g, at], s_ss.at[k, h], s_rs.at[g, h], pdev(ppeer[k])))

    def factors(h):
        at = half(h)
        st = stats[g, at]

        def add_factor(m, acc):
            block = pin_v[pl.ds(pl.multiple_of(m * slice_w, 128), slice_w), :]
            normed = norm(zbuf[m, at], st[:, 0:1], st[:, 64:65], zgain[m])
            return acc + jnp.dot(normed, block, preferred_element_type=f32)

        factor = lax.fori_loop(0, N, add_factor, jnp.zeros((HALVES[h][1], pin_v.shape[1]), f32))
        term_out[at] = jnp.dot(factor.astype(bf16), pout_v[...], preferred_element_type=f32).astype(bf16)
        terms[n, at] = term_out[at]
        for k in range(1, N):
            go(send(term_out.at[at], terms.at[n, at], t_ss.at[k, h], t_rs.at[n, h], zdev(zpeer[k])))

    def pre_send(k, q, h):
        at = half(h)
        return send(pre_out.at[q, at], pre_in.at[g, at], p_ss.at[lax.rem(k, N), h], p_rs.at[g, h], pdev(q))

    def ups(h):
        at = half(h)

        def up(k, _):
            q = plane(k)

            @pl.when(k < N)
            def _():
                for c in HALVES[h][2]:
                    send(x_ref.at[rows(c)], xin.at[q, rows(c)], x_ss.at[1, c], x_rs.at[q, c], pdev(q)).wait_recv()
                send(stats.at[g, at], stats.at[q, at], s_ss.at[1, h], s_rs.at[q, h], pdev(q)).wait_recv()

            st = stats[q, at]
            normed = norm(xin[q, at], st[:, 0:1], st[:, 64:65], zgain[g])
            pre_out[q, at] = jnp.dot(normed, picked(up_v, q), preferred_element_type=f32).astype(bf16)

            @pl.when(k < N)
            def _():
                pre_send(k, q, h).start()

            return 0

        lax.fori_loop(1, N + 1, up, 0)
        for k in range(1, N):
            sent.append(pre_send(jnp.int32(k), ppeer[k], h))

    def hiddens(h):
        at = half(h)
        for k in range(1, N):
            m = zpeer[k]
            send(term_out.at[at], terms.at[m, at], t_ss.at[1, h], t_rs.at[m, h], zdev(m)).wait_recv()
        scores = jnp.zeros((HALVES[h][1], 128), f32)
        for m in range(N):
            scores = scores + terms[m, at].astype(f32)
        gates = jax.nn.sigmoid(scores)
        mine = chosen(g)
        gate = [jnp.sum(gates * pick_v[i], axis=1, keepdims=True) for i in mine]
        bias = [bias_v[jnp.minimum(i, blocks - 1)] for i in mine]
        pre = pre_out[g, at].astype(f32)
        for k in range(1, N):
            q = ppeer[k]
            send(pre_out.at[g, at], pre_in.at[q, at], p_ss.at[1, h], p_rs.at[q, h], pdev(q)).wait_recv()
            pre = pre + pre_in[q, at].astype(f32)
        hidden = [
            (jnp.maximum(pre[:, j * BW : (j + 1) * BW] + bias[j], 0.0) * gate[j]).astype(bf16)
            for j in range(2)
        ]
        hid[g, at] = jnp.concatenate(hidden, axis=1)
        for k in range(1, N):
            go(send(hid.at[g, at], hid.at[g, at], h_ss.at[k, h], h_rs.at[g, h], pdev(ppeer[k])))

    def outward(k, c):
        q = ppeer[k]
        return send(outp.at[q, rows(c)], pbuf.at[g, rows(c)], o_ss.at[k, c], o_rs.at[g, c], pdev(q))

    def downs(h):
        at = half(h)

        def down(k, _):
            q = plane(k)

            @pl.when(k < N)
            def _():
                send(hid.at[g, at], hid.at[q, at], h_ss.at[1, h], h_rs.at[q, h], pdev(q)).wait_recv()

            outp[q, at] = lax.dot_general(
                hid[q, at], picked(down_v, q), (((1,), (1,)), ((), ())), preferred_element_type=f32
            ).astype(bf16)
            return 0

        lax.fori_loop(1, 3, down, 0)
        for c in HALVES[h][2]:
            for k in (1, 2):
                go(outward(k, c))
        lax.fori_loop(3, N + 1, down, 0)
        for c in HALVES[h][2]:
            go(outward(3, c))
        pbuf[g, at] = outp[g, at]

    def rise(m, c, up):
        at = pbuf.at[m, rows(c)]
        if up:
            return send(at, rup.at[m, rows(c)], u_ss.at[m, c], u_rs.at[m, c], zdev(n + 1))
        return send(at, rdn.at[m, rows(c)], d_ss.at[m, c], d_rs.at[m, c], zdev(n - 1))

    def landed(m, c, up):
        buf, sems = (rup, u_rs) if up else (rdn, d_rs)
        send(x_ref.at[rows(c)], buf.at[m, rows(c)], u_ss.at[m, c], sems.at[m, c], zdev(zpeer[1])).wait_recv()

    def own(m, c):
        def wait():
            send(outp.at[0, rows(c)], pbuf.at[m, rows(c)], o_ss.at[1, c], o_rs.at[m, c], pdev(ppeer[1])).wait_recv()

        guarded(m != g, wait)

    def rises(far, h):
        for c in HALVES[h][2]:
            for up in (True, False):
                m = n + far if up else n - far

                def forward(m=m, c=c, up=up):
                    own(m, c)

                    def add():
                        landed(m, c, up)
                        other = rup if up else rdn
                        pbuf[m, rows(c)] = (
                            pbuf[m, rows(c)].astype(f32) + other[m, rows(c)].astype(f32)
                        ).astype(bf16)

                    guarded(n > 0 if up else n < N - 1, add)
                    rise(m, c, up).start()

                guarded(m < N if up else m >= 0, forward)
    for far in range(1, N):
        arrivals(far, 0)
    for k in range(1, N):
        m = zpeer[k]
        send(gain_ref, zgain.at[m], g_ss.at[1], g_rs.at[m], zdev(m)).wait_recv()

    stats_of(0)
    wait_loads(0)
    pout_v[...] = jnp.zeros(pout_v.shape, bf16)
    pout_v[:, : pout_in.shape[1]] = pout_in[...]
    arrivals(1, 1)
    factors(0)
    wait_loads(1)
    ups(0)
    arrivals(2, 1)
    hiddens(0)
    wait_loads(2)
    arrivals(3, 1)
    stats_of(1)
    downs(0)
    factors(1)
    rises(3, 0)
    ups(1)
    rises(2, 0)
    hiddens(1)
    rises(1, 0)
    downs(1)
    for far in (3, 2, 1):
        rises(far, 1)
    for c in chunks:
        own(n, c)

        def middle(c=c):
            landed(n, c, True)
            landed(n, c, False)
            total = rup[n, rows(c)].astype(f32) + rdn[n, rows(c)].astype(f32) + pbuf[n, rows(c)].astype(f32)
            out_ref[rows(c)] = (x_ref[rows(c)].astype(f32) + total).astype(bf16)

        def edge(c=c, up=True):
            landed(n, c, up)
            other = rup if up else rdn
            total = other[n, rows(c)].astype(f32) + pbuf[n, rows(c)].astype(f32)
            out_ref[rows(c)] = (x_ref[rows(c)].astype(f32) + total).astype(bf16)

        guarded(n == 0, lambda c=c: edge(c, False))
        guarded(n == N - 1, lambda c=c: edge(c, True))
        guarded((n > 0) & (n < N - 1), middle)
    for c in chunks:
        for m in range(N):
            guarded((n >= m) & (n < N - 1), lambda m=m, c=c: hop(m, c, True, x_ref.at[rows(c)]).wait_send())
            guarded((n <= m) & (n > 0), lambda m=m, c=c: hop(m, c, False, x_ref.at[rows(c)]).wait_send())
            guarded(g != m, lambda m=m, c=c: inward(m, c, x_ref.at[rows(c)]).wait_send())
            guarded(n < m, lambda m=m, c=c: rise(m, c, True).wait_send())
            guarded(n > m, lambda m=m, c=c: rise(m, c, False).wait_send())
    for copy in sent:
        copy.wait_send()


def fused_device(
    features, ln_gain, up_weight, up_bias, down_weight, pred_in, pred_out, active, counts
):
    blocks = up_weight.shape[1] // BW
    height, slice_w = features.shape
    vmem = pl.BlockSpec(memory_space=pltpu.VMEM)
    hbm = pl.BlockSpec(memory_space=pl.ANY)
    nc = len(PARTS)
    bf16, f32 = jnp.bfloat16, jnp.float32
    dma = pltpu.SemaphoreType.DMA
    return pl.pallas_call(
        layer_kernel,
        out_shape=jax.ShapeDtypeStruct(features.shape, bf16),
        in_specs=[pl.BlockSpec(memory_space=pltpu.SMEM)] * 2 + [vmem] * 2 + [hbm] * 4,
        out_specs=vmem,
        scratch_shapes=[
            pltpu.VMEM((N, height, slice_w), bf16),
            pltpu.VMEM((N, 1, slice_w), f32),
            pltpu.VMEM((N, height, slice_w), bf16),
            pltpu.VMEM((N, height, 128), f32),
            pltpu.VMEM((N, height, 128), bf16),
            pltpu.VMEM((height, 128), bf16),
            pltpu.VMEM((N, height, CAP * BW), bf16),
            pltpu.VMEM((N, height, CAP * BW), bf16),
            pltpu.VMEM((N, height, CAP * BW), bf16),
            pltpu.VMEM((N, height, slice_w), bf16),
            pltpu.VMEM((N, height, slice_w), bf16),
            pltpu.VMEM((N, height, slice_w), bf16),
            pltpu.VMEM((N, height, slice_w), bf16),
            pltpu.VMEM((blocks, up_weight.shape[0], BW), bf16),
            pltpu.VMEM((blocks, down_weight.shape[0], BW), bf16),
            pltpu.VMEM(pred_in.shape, bf16),
            pltpu.VMEM((1, slice_w), f32),
            pltpu.VMEM((blocks, 1, BW), f32),
            pltpu.VMEM((blocks + 1, 1, 128), f32),
            pltpu.VMEM(pred_out.shape, bf16),
            pltpu.VMEM((pred_out.shape[0], 128), bf16),
            pltpu.VMEM((height, 1), f32),
            pltpu.VMEM((height, 1), f32),
            dma((N, nc, 2)), dma((N, nc)),
            dma((N,)), dma((N,)),
            dma((N, nc)), dma((N, nc)),
            dma((N, 2)), dma((N, 2)),
            dma((N, 2)), dma((N, 2)),
            dma((N, 2)), dma((N, 2)),
            dma((N, 2)), dma((N, 2)),
            dma((N, nc)), dma((N, nc)),
            dma((N, nc)), dma((N, nc)),
            dma((N, nc)), dma((N, nc)),
            dma((3, blocks)),
        ],
        compiler_params=pltpu.CompilerParams(
            collective_id=0, has_side_effects=True, vmem_limit_bytes=50 * 1024 * 1024
        ),
    )(
        active, counts, features, jnp.concatenate((ln_gain, up_bias)).reshape(1, -1), pred_out,
        up_weight, down_weight, pred_in,
    )


def solution(mesh):
    placed = (
        P(("groups", "row", "sub"), "neuron"),
        P("neuron"),
        P(("row", "sub"), "neuron"),
        P("neuron"),
        P(("row", "sub"), "neuron"),
        P(None, "neuron"),
        P("neuron", None),
        P("groups", None),
        P("groups"),
    )
    small = mesh.shape["neuron"] == N and mesh.shape["row"] == 2 and mesh.shape["sub"] == 2
    return jax.shard_map(
        fused_device if small else per_device,
        mesh=mesh,
        in_specs=placed,
        out_specs=P(("groups", "row", "sub"), "neuron"),
        check_vma=False,
    )
```
